512 devices in a mesh: atom: 128 (over y, z_hi, x, core), mode: 4 (over z_lo).
Axes of the slice: x: 4, y: 8, z: 8 (z_hi: 2, z_lo: 4; z = z_hi * 4 + z_lo), core: 2. Of those that a mesh axis runs over, the one named last changes fastest.
Arguments:
- velocity: bfloat16 [196608, 128], P('atom'), may hold values from -6 to 6
- local_virial: bfloat16 [196608, 384], P('atom'), may hold values from -6 to 6
- ghost_virial: bfloat16 [49152, 384], P('atom'), may hold values from -6 to 6
- eigvec: bfloat16 [196608, 4096], P('atom', 'mode'), may hold values from -0.0546875 to 0.0546875
- ghost_slot: int32 [16384], P('atom'), may hold values from 0 to 127, as said below
- counts: int32 [128], P('atom'), may hold values from 128 to 512, as said below
Outputs:
- modal_current: float32 [4, 1024, 3, 128], P('mode', 'atom')
- modal_corr: float32 [4, 1024, 64], P('mode', 'atom')
- slab_corr: float32 [64], replicated
The draws below stay inside these ranges and needn't reach their ends.
Inputs may be any that keep to these rules, and one draw needn't show every extreme that they name: `ghost_slot`: for each domain the first 64 ghost slots are a permutation of 64 to 127 and the last 64 a permutation of 0 to 63. `counts`: every draw has a domain with 512 atoms and one with 128.
All inputs are finite; a program needn't handle non-finite values.
Results may differ from the reference program's by a relative error of at most 0.0003.
Values may be sent and summed in bfloat16 or wider, within the bound.
A program may use at most 64 MiB of HBM per device.

```python
import math
import jax
import jax.numpy as jnp
from jax import lax

MODES = 4096
ATOM_DEV = 512
FRAMES = 128
LAGS = 64
RIM = 64
GHOST_DEV = 128
DOMAINS = 128
ATOMS = 65536
GHOSTS = 16384
BLOCK = 1024
N_MODE = 4


def draw_ghost_slot(key, part):
    key = jax.random.fold_in(key, 11)
    many_keys = jax.random.split(key, 2 * DOMAINS)
    orders = jax.vmap(lambda single: jax.random.permutation(single, RIM))(many_keys)
    orders = orders.astype(jnp.int32).reshape(DOMAINS, 2, RIM)
    lower_part = orders[:, 0, :] + RIM
    upper_part = orders[:, 1, :]
    return jnp.concatenate([lower_part, upper_part], axis=1).reshape(GHOSTS).astype(jnp.int32)


def draw_counts(key, part):
    key = jax.random.fold_in(key, 7)
    first_key, second_key = jax.random.split(key)
    filled = jax.random.randint(first_key, (DOMAINS,), 2 * RIM, ATOM_DEV + 1, dtype=jnp.int32)
    fullest = jax.random.randint(second_key, (), 0, DOMAINS, dtype=jnp.int32)
    filled = filled.at[fullest].set(ATOM_DEV)
    filled = filled.at[(fullest + 1) % DOMAINS].set(2 * RIM)
    return filled.astype(jnp.int32)


def with_spikes(entries, own_key, source, target, blocks, factor):
    owner, partner = [(jnp.arange(entries.shape[axis_at]) // (entries.shape[axis_at] // blocks)).reshape([-1 if axis == axis_at else 1 for axis in range(entries.ndim)]) for axis_at in (source, target)]
    chosen = jax.random.permutation(own_key, blocks)[partner]
    strong = (owner == chosen) | (owner == (partner + blocks // 2) % blocks)
    return jnp.where(strong, factor * entries, entries)


def block_levels(key, shape, cuts, smallest, largest):
    gain, own = 1.0, jax.random.fold_in(key, 6)
    for position, blocks in cuts:
        steps = jnp.exp(jax.random.uniform(jax.random.fold_in(own, position), (blocks,), jnp.float32, smallest / len(cuts), largest / len(cuts)))
        gain = gain * jnp.repeat(steps, shape[position] // blocks).reshape([-1 if axis == position else 1 for axis in range(len(shape))])
    return gain


def noise(rng, shape, spread, most, shards=(), held_as=jnp.bfloat16):
    values = jax.random.normal(rng, shape, jnp.float32) * spread
    if len(shards) > 0:
        values = block_levels(rng, shape, shards, -0.22, 0.18) * values
    return jnp.clip(values, min=-most, max=most).astype(held_as)


def bell_draw_with(stream_key, extent, deviation, most, pieces, heavy, kind=jnp.bfloat16):
    entries = deviation * jax.random.normal(stream_key, extent, jnp.float32)
    if pieces:
        entries = entries * block_levels(stream_key, extent, pieces, -0.22, 0.18)
    return jnp.clip(with_spikes(entries, jax.random.fold_in(stream_key, 3), *heavy), -most, most).astype(kind)


def setup_inputs(seed: int = 0) -> dict:
    seeds = jax.random.split(jax.random.key(seed), 7)
    velocity = noise(seeds[0], (3 * ATOMS, FRAMES), 1.0, 6.0, ((0, 128),))
    local_virial = noise(seeds[1], (3 * ATOMS, 3 * FRAMES), 1.0, 6.0, ((0, 128),))
    ghost_virial = noise(seeds[2], (3 * GHOSTS, 3 * FRAMES), 0.7, 6.0, ((0, 128),))
    eigvec = bell_draw_with(seeds[3], (3 * ATOMS, MODES), (3 * ATOMS) ** -0.5, 0.0546875, ((0, 128), (1, 4)), (0, 1, 128, 5.5))
    ghost_slot = draw_ghost_slot(jax.random.fold_in(seeds[6], 71), 0)
    counts = draw_counts(jax.random.fold_in(seeds[6], 71), 0)
    return {"velocity": velocity, "local_virial": local_virial, "ghost_virial": ghost_virial, "eigvec": eigvec, "ghost_slot": ghost_slot, "counts": counts}


def reference(velocity, local_virial, ghost_virial, eigvec, ghost_slot, counts):
    row_ids = jnp.arange(3 * ATOMS, dtype=jnp.int32)
    slot_ids = row_ids // 3 % ATOM_DEV
    domain_ids = row_ids // (3 * ATOM_DEV)
    alive_rows = (slot_ids < counts[domain_ids]).astype(jnp.bfloat16)[:, None]
    moving = velocity * alive_rows
    stress = local_virial * alive_rows
    ghost_ids = jnp.arange(GHOSTS, dtype=jnp.int32)
    ghost_domain = ghost_ids // GHOST_DEV
    ghost_place = ghost_ids % GHOST_DEV
    owner_domain = jnp.where(ghost_place < RIM, (ghost_domain - 1) % DOMAINS, (ghost_domain + 1) % DOMAINS)
    owner_atom = (owner_domain * ATOM_DEV + ghost_slot).astype(jnp.int32)
    owner_rows = (owner_atom[:, None] * 3 + jnp.arange(3, dtype=jnp.int32)[None, :]).reshape(-1)
    ghost_modes = eigvec[owner_rows]
    ghost_speed = velocity[owner_rows]
    xdot = jnp.dot(moving.T, eigvec, preferred_element_type=jnp.float32)
    proj = jnp.dot(stress.T, eigvec, preferred_element_type=jnp.float32)
    proj = proj + jnp.dot(ghost_virial.T, ghost_modes, preferred_element_type=jnp.float32)
    flux = xdot[None, :, :] * proj.reshape(3, FRAMES, MODES)
    modal_flux = jnp.transpose(flux, (2, 0, 1))
    stress_f = stress.astype(jnp.float32).reshape(3 * ATOMS, 3, FRAMES)
    moving_f = moving.astype(jnp.float32)
    current_sum = lax.optimization_barrier(jnp.sum(stress_f * moving_f[:, None, :], axis=0))
    ghost_f = ghost_virial.astype(jnp.float32).reshape(3 * GHOSTS, 3, FRAMES)
    current_sum = current_sum + lax.optimization_barrier(jnp.sum(ghost_f * ghost_speed.astype(jnp.float32)[:, None, :], axis=0))
    current_sum = current_sum / math.sqrt(ATOMS)
    padded = jnp.concatenate([current_sum, jnp.zeros((3, LAGS), jnp.float32)], axis=1)
    lag_index = jnp.arange(FRAMES, dtype=jnp.int32)[:, None] + jnp.arange(LAGS, dtype=jnp.int32)[None, :]
    hankel = padded[:, lag_index]
    lag_corr = jnp.einsum('nbt,btl->nl', modal_flux, hankel, precision=lax.Precision.HIGHEST)
    lag_corr = lag_corr / (FRAMES - jnp.arange(LAGS)).astype(jnp.float32)[None, :]
    slab_sum = lax.optimization_barrier(jnp.sum(lag_corr, axis=0)) / math.sqrt(MODES)
    return (modal_flux.reshape(N_MODE, BLOCK, 3, FRAMES), lag_corr.reshape(N_MODE, BLOCK, LAGS), slab_sum)
```

```python
import functools
import math

import jax
import jax.numpy as jnp
from jax import lax
from jax.experimental import pallas as pl
from jax.experimental.pallas import tpu as pltpu
from jax.sharding import PartitionSpec as P

MESH = pl.DeviceIdType.MESH
F32 = jnp.float32
BF16 = jnp.bfloat16
HIGHEST = lax.Precision.HIGHEST
NY, NH, NX, NC, NM = 8, 2, 4, 2, 4
T = 128
K = 8
FACE = 192
LAGS = 64


def dot_rows(left, right):
    return lax.dot_general(left, right, (((0,), (0,)), ((), ())), preferred_element_type=F32)


def iota(shape, dim):
    return lax.broadcasted_iota(jnp.int32, shape, dim)


def placing(slots, face):
    ghost = iota((T, FACE), 0) - 64 * face
    third = lax.shift_right_logical(iota((T, FACE), 1) * 171, 9)
    spread = jnp.where(ghost == third, 1.0, 0.0).astype(BF16)
    base = 64 if face == 0 else 0
    slot = (slots - base).astype(F32).astype(BF16)
    slot = jnp.dot(jnp.broadcast_to(slot, (8, T)), spread, preferred_element_type=F32)
    lane = iota((8, FACE), 1)
    third = lax.shift_right_logical(lane * 171, 9)
    target = 3 * slot.astype(jnp.int32) + (lane - 3 * third)
    return jnp.where(iota((FACE, FACE), 0) == target[0:1, :], 1.0, 0.0).astype(BF16)


def hankel(total):
    parts = []
    for b in range(3):
        row = jnp.concatenate([total[b : b + 1, :], jnp.zeros((1, T), F32)], axis=1)
        row = jnp.broadcast_to(row, (T, 2 * T))
        parts.append(pltpu.roll(row, T + 1, 1, stride=1, stride_axis=0)[:, :T])
    flipped = jnp.concatenate(parts, axis=1)
    flip = jnp.where(iota((T, T), 0) + iota((T, T), 1) == T - 1, 1.0, 0.0).astype(F32)
    return jnp.dot(flip, flipped, precision=HIGHEST, preferred_element_type=F32)


def correlate(parts, lagged):
    out = None
    for b in range(3):
        term = jnp.dot(
            parts[b], lagged[:, b * T : (b + 1) * T], precision=HIGHEST, preferred_element_type=F32
        )
        out = term if out is None else out + term
    return out / (T - iota(out.shape, 1)).astype(F32)


def kernel(
    vel, vir, gho, eig, slots, counts, flux_out, corr_out, slab_out,
    ev, ms, gv, sv, placed, gh, part, cr, cs, ry, rx, x1, ry2, y1, rx2, zz, rh,
    tp, tc, tx, ty, th, sz, sy, sx,
    load_sem, gh_s, gh_r, c_s, c_r, rx_s, rx_r, ry_s, ry_r, ry2_s, ry2_r, rx2_s, rx2_r, h_s, h_r,
    t_s, t_r, sz_s, sz_r, sy_s, sy_r, sx_s, sx_r,
):
    a = lax.axis_index("atom")
    m = lax.axis_index("mode")
    c, x, h, y = lax.rem(a, 2), lax.rem(lax.div(a, 2), 4), lax.rem(lax.div(a, 8), 2), lax.div(a, 16)
    place = lax.rem(a, 8)

    def dev(y=y, h=h, x=x, c=c, m=m):
        return (((y * NH + h) * NX + x) * NC + c, m)

    core = dev(c=1 - c)
    x_peers = [lax.rem(x + k, NX) for k in range(1, NX)]
    y_peers = [lax.rem(y + k, NY) for k in range(1, NY)]
    z_peers = [
        (lax.rem(h + i // 8, NH), lax.rem(m + (i // 2) % 4, NM), lax.rem(c + i % 2, NC))
        for i in range(1, 16)
    ]
    h_peer = dev(h=1 - h)
    domains = NY * NH * NX * NC
    above, below = lax.rem(a + 1, domains), lax.rem(a + domains - 1, domains)
    up_far, down_far = place == 7, place == 0
    edge = jnp.logical_or(m == 0, m == 3)
    far_source = jnp.where(m < 2, 3, 0)
    far_first = jnp.where(m == 3, 0, 2)

    loads = [
        pltpu.make_async_copy(slots, sv, load_sem.at[0]),
        pltpu.make_async_copy(gho, gv, load_sem.at[1]),
        pltpu.make_async_copy(vel, ms.at[:, 0:T], load_sem.at[2]),
        pltpu.make_async_copy(vir, ms.at[:, T:], load_sem.at[3]),
    ]
    loads += [
        pltpu.make_async_copy(
            eig.at[pl.ds(192 * i, 192)], ev.at[pl.ds(192 * i, 192)], load_sem.at[4 + i]
        )
        for i in range(8)
    ]

    barrier = pltpu.get_barrier_semaphore()

    def greet(device):
        pl.semaphore_signal(barrier, 1, device_id=device, device_id_type=MESH)

    greet((below, jnp.where(down_far, far_source, m)))
    greet((above, jnp.where(up_far, far_source, m)))
    for xx in x_peers:
        greet(dev(x=xx))
    for yy in y_peers:
        greet(dev(y=yy))
    for hh, mm, cc in z_peers:
        greet(dev(h=hh, m=mm, c=cc))
    for load in loads:
        load.start()

    def ghost_sends():
        for side, (far, there) in enumerate(((up_far, above), (down_far, below))):
            first = jnp.where(far, far_first, m)
            once = jnp.logical_or(jnp.logical_not(far), edge)
            twice = jnp.logical_and(far, edge)
            for n, (when, mode) in enumerate(((once, first), (twice, far_first + 1))):
                yield when, pltpu.make_async_remote_copy(
                    src_ref=placed.at[side],
                    dst_ref=gh.at[side],
                    send_sem=gh_s.at[side, n],
                    recv_sem=gh_r.at[side],
                    device_id=(there, mode),
                    device_id_type=MESH,
                )

    sends = []

    def put(src, dst, send_sem, recv_sem, device):
        copy = pltpu.make_async_remote_copy(
            src_ref=src, dst_ref=dst, send_sem=send_sem, recv_sem=recv_sem,
            device_id=device, device_id_type=MESH,
        )
        copy.start()
        sends.append(copy)

    def arrived(dst, send_sem, recv_sem):
        pltpu.make_async_remote_copy(
            src_ref=dst, dst_ref=dst, send_sem=send_sem, recv_sem=recv_sem,
            device_id=core, device_id_type=MESH,
        ).wait_recv()

    loads[0].wait()
    loads[1].wait()
    for face in range(2):
        rows = jnp.dot(
            placing(sv[...], face), gv[FACE * face : FACE * (face + 1), :], preferred_element_type=F32
        )
        placed[1 - face] = rows.astype(BF16)
    sent_ghosts = 2 * jnp.ones((), jnp.int32)
    far = jnp.logical_or(up_far, down_far)
    sent_ghosts = jnp.where(far, jnp.where(edge, 3, 1), 2)
    pl.semaphore_wait(barrier, 3 + 7 + 15 + sent_ghosts)
    for when, copy in ghost_sends():
        pl.when(when)(copy.start)

    for load in loads[2:4]:
        load.wait()
    alive = jnp.where(iota((ms.shape[0], T), 0) < 3 * counts[0], 1.0, 0.0).astype(BF16)
    for q in range(4):
        ms[:, q * T : (q + 1) * T] = ms[:, q * T : (q + 1) * T] * alive
    for load in loads[4:]:
        load.wait()
    order = [lax.rem(lax.div(y, 2) + k, 4) for k in (1, 2, 3, 0)]
    for j in order:
        cols = pl.ds(pl.multiple_of(j * 256, 256), 256)
        acc = dot_rows(ev[:, cols], ms[...])
        for q in range(4):
            part[q, pl.ds(2 * j, 2)] = acc[:, q * T : (q + 1) * T].reshape(2, NH, NX, NC, K, T)
    total = dot_rows(ms[:, :T], ms[:, T:])

    for side in range(2):
        arrived(gh.at[side], gh_s.at[side, 0], gh_r.at[side])
    ghosts = gh[...].reshape(2 * FACE, 3 * T)
    total = total + dot_rows(ms[: 2 * FACE, :T], ghosts)
    diagonal = iota((T, T), 0) == iota((T, T), 1)
    tp[...] = jnp.concatenate(
        [
            jnp.sum(jnp.where(diagonal, total[:, b * T : (b + 1) * T], 0.0), axis=0, keepdims=True)
            for b in range(3)
        ]
        + [jnp.zeros((5, T), F32)],
        axis=0,
    )
    put(tp, tc, t_s.at[0], t_r.at[0], core)
    for k, j in enumerate(order):
        cols = pl.ds(pl.multiple_of(j * 256, 256), 256)
        acc = dot_rows(ev[: 2 * FACE, cols], ghosts)
        for q in range(1, 4):
            now = acc[:, (q - 1) * T : q * T].reshape(2, NH, NX, NC, K, T)
            part[q, pl.ds(2 * j, 2)] = part[q, pl.ds(2 * j, 2)] + now
        put(
            part.at[:, pl.ds(2 * j, 2), :, :, 1 - c], cr.at[:, pl.ds(2 * j, 2)],
            c_s.at[k], c_r.at[k], core,
        )

    arrived(tc, t_s.at[0], t_r.at[0])
    tx[x] = tp[...] + tc[...]
    for k, xx in enumerate(x_peers):
        put(tx.at[x], tx.at[x], t_s.at[1 + k], t_r.at[1 + x], dev(x=xx))
    for k, j in enumerate(order):
        two = pl.ds(2 * j, 2)
        arrived(cr.at[:, two], c_s.at[k], c_r.at[k])
        cs[:, two] = part[:, two, :, :, c] + cr[:, two]
        for n, xx in enumerate(x_peers):
            put(cs.at[2:4, two, :, xx], rx.at[n, :, two], rx_s.at[n, k], rx_r.at[n, k], dev(x=xx))
        targets = [2 * j, 2 * j + 1] if k < 3 else [y + 1 - 2 * lax.rem(y, 2)]
        for n, yy in enumerate(targets):
            put(cs.at[0:2, yy], ry.at[y], ry_s.at[2 * k + n], ry_r.at[y], dev(y=yy))
    for xx in x_peers:
        arrived(tx.at[xx], t_s.at[0], t_r.at[1 + xx])
    ty[y] = ((tx[0] + tx[1]) + tx[2]) + tx[3]
    for k, yy in enumerate(y_peers):
        put(ty.at[y], ty.at[y], t_s.at[4 + k], t_r.at[5 + y], dev(y=yy))
    for k, j in enumerate(order):
        two = pl.ds(2 * j, 2)
        for n in range(3):
            arrived(rx.at[n, :, two], rx_s.at[n, k], rx_r.at[n, k])
        x1[:, two] = (cs[2:4, two, :, x] + rx[0, :, two]) + (rx[1, :, two] + rx[2, :, two])
        targets = [2 * j, 2 * j + 1] if k < 3 else [y + 1 - 2 * lax.rem(y, 2)]
        for n, yy in enumerate(targets):
            put(x1.at[:, yy], ry2.at[y], ry2_s.at[2 * k + n], ry2_r.at[y], dev(y=yy))
    summed = cs[0:2, y]
    for yy in y_peers:
        arrived(ry.at[yy], ry_s.at[0], ry_r.at[yy])
        summed = summed + ry[yy]
    y1[...] = summed
    for n, xx in enumerate(x_peers):
        put(y1.at[:, :, xx], rx2.at[n], rx2_s.at[n], rx2_r.at[n], dev(x=xx))
    for yy in y_peers:
        arrived(ty.at[yy], t_s.at[0], t_r.at[5 + yy])
    summed = ty[0]
    for n in range(1, NY):
        summed = summed + ty[n]
    th[0] = summed
    put(th.at[0], th.at[1], t_s.at[11], t_r.at[13], h_peer)

    summed = x1[:, y]
    for yy in y_peers:
        arrived(ry2.at[yy], ry2_s.at[0], ry2_r.at[yy])
        summed = summed + ry2[yy]
    zz[2:4] = summed
    summed = y1[:, :, x]
    for n in range(3):
        arrived(rx2.at[n], rx2_s.at[n], rx2_r.at[n])
        summed = summed + rx2[n]
    zz[0:2] = summed
    put(zz.at[:, 1 - h], rh, h_s, h_r, h_peer)
    arrived(th.at[1], t_s.at[0], t_r.at[13])
    lagged = hankel((th[0] + th[1]) * (1.0 / math.sqrt(ms.shape[0] // 3 * domains)))
    arrived(rh, h_s, h_r)
    final = zz[:, h] + rh[...]
    flux = [final[0] * final[1 + b] for b in range(3)]

    here = (h * NM + m) * NC + c
    sz[here] = jnp.concatenate(
        [jnp.sum(flux[b], axis=0, keepdims=True) for b in range(3)] + [jnp.zeros((5, T), F32)], axis=0
    )
    for n, (hh, mm, cc) in enumerate(z_peers):
        put(sz.at[here], sz.at[here], sz_s.at[n], sz_r.at[here], dev(h=hh, m=mm, c=cc))
    for b in range(3):
        flux_out[0, :, b, :] = flux[b]
    corr_out[0] = correlate(flux, lagged)[:, :LAGS]
    for hh, mm, cc in z_peers:
        there = (hh * NM + mm) * NC + cc
        arrived(sz.at[there], sz_s.at[0], sz_r.at[there])
    summed = sz[0]
    for n in range(1, 16):
        summed = summed + sz[n]
    sy[y] = summed
    for k, yy in enumerate(y_peers):
        put(sy.at[y], sy.at[y], sy_s.at[k], sy_r.at[y], dev(y=yy))
    for yy in y_peers:
        arrived(sy.at[yy], sy_s.at[0], sy_r.at[yy])
    summed = sy[0]
    for n in range(1, NY):
        summed = summed + sy[n]
    sx[x] = summed
    for k, xx in enumerate(x_peers):
        put(sx.at[x], sx.at[x], sx_s.at[k], sx_r.at[x], dev(x=xx))
    for xx in x_peers:
        arrived(sx.at[xx], sx_s.at[0], sx_r.at[xx])
    slab = ((sx[0] + sx[1]) + sx[2]) + sx[3]
    slab = correlate([jnp.broadcast_to(slab[b : b + 1, :], (8, T)) for b in range(3)], lagged)
    slab_out[...] = slab[0:1, :LAGS] * (1.0 / math.sqrt(NM * domains * K))

    for copy in sends:
        copy.wait_send()
    for when, copy in ghost_sends():
        pl.when(when)(copy.wait_send)


def per_device(velocity, local_virial, ghost_virial, eigvec, ghost_slot, counts):
    rows, modes = eigvec.shape
    vmem = pltpu.VMEM
    dma = pltpu.SemaphoreType.DMA
    scratch = [
        vmem((rows, modes), BF16),
        vmem((rows, 4 * T), BF16),
        vmem((2 * FACE, 3 * T), BF16),
        vmem((1, T), jnp.int32),
        vmem((2, FACE, 3 * T), BF16),
        vmem((2, FACE, 3 * T), BF16),
        vmem((4, NY, NH, NX, NC, K, T), F32),
        vmem((4, NY, NH, NX, K, T), F32),
        vmem((4, NY, NH, NX, K, T), F32),
        vmem((NY, 2, NH, NX, K, T), F32),
        vmem((3, 2, NY, NH, K, T), F32),
        vmem((2, NY, NH, K, T), F32),
        vmem((NY, 2, NH, K, T), F32),
        vmem((2, NH, NX, K, T), F32),
        vmem((3, 2, NH, K, T), F32),
        vmem((4, NH, K, T), F32),
        vmem((4, K, T), F32),
        vmem((8, T), F32),
        vmem((8, T), F32),
        vmem((NX, 8, T), F32),
        vmem((NY, 8, T), F32),
        vmem((2, 8, T), F32),
        vmem((16, 8, T), F32),
        vmem((NY, 8, T), F32),
        vmem((NX, 8, T), F32),
        dma((12,)),
        dma((2, 2)), dma((2,)),
        dma((4,)), dma((4,)),
        dma((3, 4)), dma((3, 4)),
        dma((8,)), dma((8,)),
        dma((8,)), dma((8,)),
        dma((3,)), dma((3,)),
        dma, dma,
        dma((12,)), dma((14,)),
        dma((15,)), dma((16,)),
        dma((7,)), dma((8,)),
        dma((3,)), dma((4,)),
    ]
    anywhere = pl.BlockSpec(memory_space=pl.ANY)
    in_vmem = pl.BlockSpec(memory_space=vmem)
    flux, corr, slab = pl.pallas_call(
        kernel,
        out_shape=(
            jax.ShapeDtypeStruct((1, K, 3, T), F32),
            jax.ShapeDtypeStruct((1, K, LAGS), F32),
            jax.ShapeDtypeStruct((1, LAGS), F32),
        ),
        in_specs=[anywhere] * 5 + [pl.BlockSpec(memory_space=pltpu.SMEM)],
        out_specs=(in_vmem, in_vmem, in_vmem),
        scratch_shapes=scratch,
        compiler_params=pltpu.CompilerParams(
            collective_id=0, has_side_effects=True, vmem_limit_bytes=56 * 2**20
        ),
        name="green_kubo",
    )(velocity, local_virial, ghost_virial, eigvec, ghost_slot.reshape(1, T), counts)
    return flux, corr, slab.reshape(LAGS)


def solution(mesh):
    return jax.shard_map(
        per_device,
        mesh=mesh,
        in_specs=(
            P("atom", None),
            P("atom", None),
            P("atom", None),
            P("atom", "mode"),
            P("atom"),
            P("atom"),
        ),
        out_specs=(P("mode", "atom", None, None), P("mode", "atom", None), P()),
        check_vma=False,
    )
```

```python
import functools
import math

import jax
import jax.numpy as jnp
from jax import lax
from jax.experimental import pallas as pl
from jax.experimental.pallas import tpu as pltpu
from jax.sharding import PartitionSpec as P

MESH = pl.DeviceIdType.MESH
F32 = jnp.float32
BF16 = jnp.bfloat16
HIGHEST = lax.Precision.HIGHEST
NY, NH, NX, NC, NM = 8, 2, 4, 2, 4
T = 128
K = 8
FACE = 192
LAGS = 64


def dot_rows(left, right):
    return lax.dot_general(left, right, (((0,), (0,)), ((), ())), preferred_element_type=F32)


def iota(shape, dim):
    return lax.broadcasted_iota(jnp.int32, shape, dim)


def placing(slots, side):
    first = 64 * (1 - side)
    lowest = 64 * side
    ghost = iota((T, FACE), 0) - first
    third = lax.shift_right_logical(iota((T, FACE), 1) * 171, 9)
    spread = jnp.where(ghost == third, 1.0, 0.0).astype(BF16)
    slot = (slots - lowest).astype(F32).astype(BF16)
    slot = jnp.dot(jnp.broadcast_to(slot, (8, T)), spread, preferred_element_type=F32)
    lane = iota((8, FACE), 1)
    third = lax.shift_right_logical(lane * 171, 9)
    target = 3 * slot.astype(jnp.int32) + (lane - 3 * third)
    return jnp.where(iota((FACE, FACE), 0) == target[0:1, :], 1.0, 0.0).astype(BF16)


def hankel(total):
    parts = []
    for b in range(3):
        row = jnp.concatenate([total[:, b * T : (b + 1) * T], jnp.zeros((1, T), F32)], axis=1)
        row = jnp.broadcast_to(row, (T, 2 * T))
        parts.append(pltpu.roll(row, T + 1, 1, stride=1, stride_axis=0)[:, :T])
    flipped = jnp.concatenate(parts, axis=1)
    flip = jnp.where(iota((T, T), 0) + iota((T, T), 1) == T - 1, 1.0, 0.0).astype(F32)
    return jnp.dot(flip, flipped, precision=HIGHEST, preferred_element_type=F32)


def correlate(parts, lagged):
    out = None
    for b in range(3):
        term = jnp.dot(
            parts[b], lagged[:, b * T : (b + 1) * T], precision=HIGHEST, preferred_element_type=F32
        )
        out = term if out is None else out + term
    return out / (T - iota(out.shape, 1)).astype(F32)


def kernel(
    vel, vir, gho, eig, slots, counts, out,
    ev, ms, nv, rs, gh, ep, vp, part, cr, cs,
    rx, x1, ry, rr, rh, ryb, y1b, rxb, rhc, h1c, rxc, x1c, ryc,
    tp, tc, tx, ty, th, sz, sp,
    load_sem, gh_s, gh_r, rs_s, rs_r, c0_s, c0_r, c_s, c_r, rx_s, rx_r, ry_s, ry_r, rh_s, rh_r,
    ryb_s, ryb_r, rxb_s, rxb_r, rhc_s, rhc_r, rxc_s, rxc_r, ryc_s, ryc_r,
    t_s, t_r, sz_s, sz_r, sp_s, sp_r, hello,
):
    a = lax.axis_index("atom")
    m = lax.axis_index("mode")
    c, x, h, y = lax.rem(a, 2), lax.rem(lax.div(a, 2), 4), lax.rem(lax.div(a, 8), 2), lax.div(a, 16)
    place = lax.rem(a, 8)

    def dev(y=y, h=h, x=x, c=c, m=m):
        return (((y * NH + h) * NX + x) * NC + c, m)

    core = dev(c=1 - c)
    h_peer = dev(h=1 - h)
    x_peers = [lax.rem(x + k, NX) for k in range(1, NX)]
    y_peers = [lax.rem(y + k, NY) for k in range(1, NY)]
    z_peers = [
        (lax.rem(h + i // 8, NH), lax.rem(m + (i // 2) % 4, NM), lax.rem(c + i % 2, NC))
        for i in range(1, 16)
    ]
    p_peers = [(lax.rem(y + i // 4, NY), lax.rem(x + i % 4, NX)) for i in range(1, 32)]
    domains = NY * NH * NX * NC
    above = (lax.rem(a + 1, domains), jnp.where(place == 7, 3 - m, m))
    below = (lax.rem(a + domains - 1, domains), jnp.where(place == 0, 3 - m, m))

    barrier = pltpu.get_barrier_semaphore()
    greeted = [above, below, h_peer] + [dev(y=lax.rem(y + k, NY)) for k in (4, 3, 5, 2, 6, 1, 7)]
    m_peers = [dev(m=lax.rem(m + k, NM)) for k in range(1, NM)]
    greeted += [dev(x=xx) for xx in x_peers] + m_peers
    for device in greeted:
        pl.semaphore_signal(barrier, 1, device_id=device, device_id_type=MESH)
    loads = [
        pltpu.make_async_copy(counts, nv, load_sem.at[0]),
        pltpu.make_async_copy(vel, ms.at[:, 0:T], load_sem.at[1]),
        pltpu.make_async_copy(vir, ms.at[:, T:], load_sem.at[2]),
    ]
    loads += [
        pltpu.make_async_copy(
            eig.at[pl.ds(192 * i, 192)], ev.at[pl.ds(192 * i, 192)], load_sem.at[3 + i]
        )
        for i in range(8)
    ]
    for load in loads:
        load.start()

    sends = []

    class Copy:
        def __init__(self, src, dst, send_sem, recv_sem, device, into=None, in_sem=None):
            self.there = pltpu.make_async_remote_copy(
                src_ref=src, dst_ref=dst, send_sem=send_sem, recv_sem=recv_sem,
                device_id=device, device_id_type=MESH,
            )
            self.there.start()
            into = dst if into is None else into
            in_sem = recv_sem if in_sem is None else in_sem
            self.back = pltpu.make_async_remote_copy(
                src_ref=into, dst_ref=into, send_sem=send_sem, recv_sem=in_sem,
                device_id=device, device_id_type=MESH,
            )
            sends.append(self.there)

        def arrive(self):
            self.back.wait_recv()

    def sent():
        for copy in sends:
            copy.wait_send()
        sends.clear()

    for load in loads[:3]:
        load.wait()
    alive = jnp.where(iota((ms.shape[0], T), 0) < 3 * nv[0], 1.0, 0.0).astype(BF16)
    for q in range(4):
        ms[:, q * T : (q + 1) * T] = ms[:, q * T : (q + 1) * T] * alive

    pl.semaphore_wait(barrier, len(greeted))
    places = [
        Copy(slots, rs.at[0], rs_s.at[0], rs_r.at[0], above),
        Copy(slots, rs.at[1], rs_s.at[1], rs_r.at[1], below),
    ]
    ghost_copies = []
    for b in range(3):
        cols = pl.ds(b * T, T)
        ghost_copies += [
            Copy(gho.at[pl.ds(FACE, FACE), cols], gh.at[b, 0], gh_s.at[b, 0], gh_r.at[b, 0], above),
            Copy(gho.at[pl.ds(0, FACE), cols], gh.at[b, 1], gh_s.at[b, 1], gh_r.at[b, 1], below),
        ]

    for load in loads[3:]:
        load.wait()
    order = [lax.rem(lax.div(y, 2) + k, 4) for k in (1, 2, 3, 0)]
    core_first = []
    for k, j in enumerate(order):
        cols = pl.ds(pl.multiple_of(j * 256, 256), 256)
        two = pl.ds(2 * j, 2)
        acc = dot_rows(ev[:, cols], ms[...])
        for q in range(4):
            part[q, two] = acc[:, q * T : (q + 1) * T].reshape(2, NH, NX, NC, K, T)
        core_first.append(
            Copy(part.at[0, two, :, :, 1 - c], cr.at[0, two], c0_s.at[k], c0_r.at[k], core)
        )

    def x_sends(b, i, k, two):
        return [
            Copy(cs.at[b, two, :, xx], rx.at[i, n, two], rx_s.at[i, n, k], rx_r.at[i, n, k], dev(x=xx))
            for n, xx in enumerate(x_peers)
        ]

    def targets(k, j):
        return [2 * j, 2 * j + 1] if k < 3 else [y + 1 - 2 * lax.rem(y, 2)]

    def y_sends(i, k, j, copies):
        two = pl.ds(2 * j, 2)
        for copy in copies:
            copy.arrive()
        own = cs[2 * i, two, :, x]
        x1[i, two] = (own + rx[i, 0, two]) + (rx[i, 1, two] + rx[i, 2, two])
        return [
            (yy, Copy(x1.at[i, yy], ry.at[i, y], ry_s.at[i, 2 * k + n], ry_r.at[i, y], dev(y=yy),
                      ry.at[i, yy], ry_r.at[i, yy]))
            for n, yy in enumerate(targets(k, j))
        ]

    def gather_y(own, slots_of, copies):
        for yy, copy in copies:
            copy.arrive()
            own = own + slots_of[yy]
        return own

    xs0 = []
    for k, j in enumerate(order):
        two = pl.ds(2 * j, 2)
        core_first[k].arrive()
        cs[0, two] = part[0, two, :, :, c] + cr[0, two]
        xs0.append(x_sends(0, 0, k, two))

    total = dot_rows(ms[:, :T], ms[:, T:])
    for side in range(2):
        places[side].arrive()
        rows = pl.ds(FACE * side, FACE)
        put = placing(rs[side], side)
        ep[rows, :] = dot_rows(put, ev[rows, :]).astype(BF16)
        vp[rows, :] = dot_rows(put, ms[rows, 0:T]).astype(BF16)

    core_rest = []
    ysb, xs2, hsc = [], [], []

    def add_ghosts(b):
        for side in range(2):
            ghost_copies[2 * (b - 1) + side].arrive()
        ghosts = gh[b - 1].reshape(2 * FACE, T)
        for k, j in enumerate(order):
            cols = pl.ds(pl.multiple_of(j * 256, 256), 256)
            two = pl.ds(2 * j, 2)
            now = dot_rows(ep[:, cols], ghosts).reshape(2, NH, NX, NC, K, T)
            part[b, two] = part[b, two] + now
            core_rest.append(
                Copy(part.at[b, two, :, :, 1 - c], cr.at[b, two], c_s.at[b - 1, k], c_r.at[b - 1, k], core)
            )

    def send_on(b):
        for k, j in enumerate(order):
            two = pl.ds(2 * j, 2)
            core_rest[4 * (b - 1) + k].arrive()
            cs[b, two] = part[b, two, :, :, c] + cr[b, two]
            if b == 1:
                for n, yy in enumerate(targets(k, j)):
                    ysb.append(
                        (yy, Copy(cs.at[1, yy], ryb.at[y], ryb_s.at[2 * k + n], ryb_r.at[y], dev(y=yy),
                                  ryb.at[yy], ryb_r.at[yy]))
                    )
            elif b == 2:
                xs2.append(x_sends(2, 1, k, two))
            else:
                hsc.append(Copy(cs.at[3, two, 1 - h], rhc.at[two], rhc_s.at[k], rhc_r.at[k], h_peer))

    add_ghosts(1)
    add_ghosts(2)
    send_on(1)
    add_ghosts(3)
    send_on(2)

    diagonal = iota((T, T), 0) == iota((T, T), 1)
    parts = []
    for b in range(3):
        now = total[:, b * T : (b + 1) * T] + dot_rows(vp[...], gh[b].reshape(2 * FACE, T))
        parts.append(jnp.sum(jnp.where(diagonal, now, 0.0), axis=0, keepdims=True))
    tp[...] = jnp.concatenate(parts, axis=1)
    tot_core = Copy(tp, tc, t_s.at[0], t_r.at[0], core)
    send_on(3)

    tot_core.arrive()
    tx[x] = tp[...] + tc[...]
    tot_x = [
        Copy(tx.at[x], tx.at[x], t_s.at[1 + k], t_r.at[1 + x], dev(x=xx), tx.at[xx], t_r.at[1 + xx])
        for k, xx in enumerate(x_peers)
    ]
    ys0 = []
    for k, j in enumerate(order):
        ys0 += y_sends(0, k, j, xs0[k])
    ys2, xsc = [], []
    for k, j in enumerate(order):
        ys2 += y_sends(1, k, j, xs2[k])
    for k, j in enumerate(order):
        two = pl.ds(2 * j, 2)
        hsc[k].arrive()
        h1c[two] = cs[3, two, h] + rhc[two]
        xsc.append(
            [
                Copy(h1c.at[two, xx], rxc.at[n, two], rxc_s.at[n, k], rxc_r.at[n, k], dev(x=xx))
                for n, xx in enumerate(x_peers)
            ]
        )
    for device in m_peers:
        pl.semaphore_signal(hello, 1, device_id=device, device_id_type=MESH)
    for copy in tot_x:
        copy.arrive()
    ty[y] = ((tx[0] + tx[1]) + tx[2]) + tx[3]
    tot_y = [
        Copy(ty.at[y], ty.at[y], t_s.at[4 + k], t_r.at[5 + y], dev(y=yy), ty.at[yy], t_r.at[5 + yy])
        for k, yy in enumerate(y_peers)
    ]
    y1b[...] = gather_y(cs[1, y], ryb, ysb)
    xsb = [
        Copy(y1b.at[:, xx], rxb.at[n], rxb_s.at[n], rxb_r.at[n], dev(x=xx))
        for n, xx in enumerate(x_peers)
    ]
    ysc = []
    for k, j in enumerate(order):
        two = pl.ds(2 * j, 2)
        for copy in xsc[k]:
            copy.arrive()
        x1c[two] = (h1c[two, x] + rxc[0, two]) + (rxc[1, two] + rxc[2, two])
        for n, yy in enumerate(targets(k, j)):
            ysc.append(
                (yy, Copy(x1c.at[yy], ryc.at[y], ryc_s.at[2 * k + n], ryc_r.at[y], dev(y=yy),
                          ryc.at[yy], ryc_r.at[yy]))
            )

    def h_send(b):
        return Copy(rr.at[b, 1 - h], rh.at[b], rh_s.at[b], rh_r.at[b], h_peer)

    rr[0] = gather_y(x1[0, y], ry.at[0], ys0)
    hs = [h_send(0)]
    for copy in tot_y:
        copy.arrive()
    summed = ty[0]
    for n in range(1, NY):
        summed = summed + ty[n]
    th[0] = summed
    tot_h = Copy(th.at[0], th.at[1], t_s.at[11], t_r.at[13], h_peer)
    rr[2] = gather_y(x1[1, y], ry.at[1], ys2)
    hs.append(h_send(2))
    summed = y1b[:, x]
    for n, copy in enumerate(xsb):
        copy.arrive()
        summed = summed + rxb[n]
    rr[1] = summed
    hs.insert(1, h_send(1))
    tot_h.arrive()
    lagged = hankel((th[0] + th[1]) * (1.0 / math.sqrt(ms.shape[0] // 3 * domains)))
    last = gather_y(x1c[y], ryc, ysc)
    final = []
    for b in range(3):
        hs[b].arrive()
        final.append(rr[b, h] + rh[b])
    final.append(last)
    flux = [final[0] * final[1 + b] for b in range(3)]

    here = (h * NM + m) * NC + c
    sz[here] = jnp.concatenate([jnp.sum(flux[b], axis=0, keepdims=True) for b in range(3)], axis=1)
    pl.semaphore_wait(hello, NM - 1)
    szs = []
    for n, (hh, mm, cc) in enumerate(z_peers):
        there = (hh * NM + mm) * NC + cc
        szs.append(
            Copy(sz.at[here], sz.at[here], sz_s.at[n], sz_r.at[here], dev(h=hh, m=mm, c=cc),
                 sz.at[there], sz_r.at[there])
        )
    for b in range(3):
        out[b] = flux[b]
    out[3] = correlate(flux, lagged)
    sent()
    for copy in szs:
        copy.arrive()
    summed = sz[0]
    for n in range(1, 16):
        summed = summed + sz[n]
    here = y * NX + x
    sp[here] = summed
    sps = []
    for n, (yy, xx) in enumerate(p_peers):
        there = yy * NX + xx
        sps.append(
            Copy(sp.at[here], sp.at[here], sp_s.at[n], sp_r.at[here], dev(y=yy, x=xx),
                 sp.at[there], sp_r.at[there])
        )
    for copy in sps:
        copy.arrive()
    slab = sp[0]
    for n in range(1, 32):
        slab = slab + sp[n]
    slab = correlate([jnp.broadcast_to(slab[:, b * T : (b + 1) * T], (8, T)) for b in range(3)], lagged)
    out[4] = slab * (1.0 / math.sqrt(NM * domains * K))
    sent()


def deliver(held, flux, corr, slab):
    flux[0] = held[0:3]
    corr[0] = held[3, :, :LAGS]
    slab[...] = held[4, 0:1, :LAGS]


def per_device(velocity, local_virial, ghost_virial, eigvec, ghost_slot, counts):
    rows, modes = eigvec.shape
    vmem = pltpu.VMEM
    dma = pltpu.SemaphoreType.DMA
    scratch = [
        vmem((rows, modes), BF16),
        vmem((rows, 4 * T), BF16),
        pltpu.SMEM((1,), jnp.int32),
        vmem((2, 1, T), jnp.int32),
        vmem((3, 2, FACE, T), BF16),
        vmem((2 * FACE, modes), BF16),
        vmem((2 * FACE, T), BF16),
        vmem((4, NY, NH, NX, NC, K, T), F32),
        vmem((4, NY, NH, NX, K, T), F32),
        vmem((4, NY, NH, NX, K, T), F32),
        vmem((2, 3, NY, NH, K, T), F32),
        vmem((2, NY, NH, K, T), F32),
        vmem((2, NY, NH, K, T), F32),
        vmem((3, NH, K, T), F32),
        vmem((3, K, T), F32),
        vmem((NY, NH, NX, K, T), F32),
        vmem((NH, NX, K, T), F32),
        vmem((3, NH, K, T), F32),
        vmem((NY, NX, K, T), F32),
        vmem((NY, NX, K, T), F32),
        vmem((3, NY, K, T), F32),
        vmem((NY, K, T), F32),
        vmem((NY, K, T), F32),
        vmem((1, 3 * T), F32),
        vmem((1, 3 * T), F32),
        vmem((NX, 1, 3 * T), F32),
        vmem((NY, 1, 3 * T), F32),
        vmem((2, 1, 3 * T), F32),
        vmem((16, 1, 3 * T), F32),
        vmem((32, 1, 3 * T), F32),
        dma((11,)),
        dma((3, 2)), dma((3, 2)),
        dma((2,)), dma((2,)),
        dma((4,)), dma((4,)),
        dma((3, 4)), dma((3, 4)),
        dma((2, 3, 4)), dma((2, 3, 4)),
        dma((2, 8)), dma((2, 8)),
        dma((3,)), dma((3,)),
        dma((8,)), dma((8,)),
        dma((3,)), dma((3,)),
        dma((4,)), dma((4,)),
        dma((3, 4)), dma((3, 4)),
        dma((8,)), dma((8,)),
        dma((12,)), dma((14,)),
        dma((15,)), dma((16,)),
        dma((31,)), dma((32,)),
        pltpu.SemaphoreType.REGULAR,
    ]
    held = pl.pallas_call(
        kernel,
        out_shape=jax.ShapeDtypeStruct((5, K, T), F32),
        in_specs=[pl.BlockSpec(memory_space=pl.ANY)] * 6,
        out_specs=pl.BlockSpec(memory_space=vmem),
        scratch_shapes=scratch,
        compiler_params=pltpu.CompilerParams(
            collective_id=0, has_side_effects=True, vmem_limit_bytes=56 * 2**20
        ),
        name="green_kubo",
    )(velocity, local_virial, ghost_virial, eigvec, ghost_slot.reshape(1, T), counts)
    flux, corr, slab = pl.pallas_call(
        deliver,
        out_shape=(
            jax.ShapeDtypeStruct((1, 3, K, T), F32),
            jax.ShapeDtypeStruct((1, K, LAGS), F32),
            jax.ShapeDtypeStruct((1, LAGS), F32),
        ),
        name="deliver",
    )(held)
    return jnp.transpose(flux, (0, 2, 1, 3)), corr, slab.reshape(LAGS)


def solution(mesh):
    return jax.shard_map(
        per_device,
        mesh=mesh,
        in_specs=(
            P("atom", None),
            P("atom", None),
            P("atom", None),
            P("atom", "mode"),
            P("atom"),
            P("atom"),
        ),
        out_specs=(P("mode", "atom", None, None), P("mode", "atom", None), P()),
        check_vma=False,
    )
```

```python
import functools
import math

import jax
import jax.numpy as jnp
from jax import lax
from jax.experimental import pallas as pl
from jax.experimental.pallas import tpu as pltpu
from jax.sharding import PartitionSpec as P

MESH = pl.DeviceIdType.MESH
F32 = jnp.float32
BF16 = jnp.bfloat16
HIGHEST = lax.Precision.HIGHEST
NY, NH, NX, NC, NM = 8, 2, 4, 2, 4
T = 128
K = 8
FACE = 192
LAGS = 64


def dot_rows(left, right):
    return lax.dot_general(left, right, (((0,), (0,)), ((), ())), preferred_element_type=F32)


def iota(shape, dim):
    return lax.broadcasted_iota(jnp.int32, shape, dim)


def placing(slots, side):
    first = 64 * (1 - side)
    lowest = 64 * side
    ghost = iota((T, FACE), 0) - first
    third = lax.shift_right_logical(iota((T, FACE), 1) * 171, 9)
    spread = jnp.where(ghost == third, 1.0, 0.0).astype(BF16)
    slot = (slots - lowest).astype(F32).astype(BF16)
    slot = jnp.dot(jnp.broadcast_to(slot, (8, T)), spread, preferred_element_type=F32)
    lane = iota((8, FACE), 1)
    third = lax.shift_right_logical(lane * 171, 9)
    target = 3 * slot.astype(jnp.int32) + (lane - 3 * third)
    return jnp.where(iota((FACE, FACE), 0) == target[0:1, :], 1.0, 0.0).astype(BF16)


def hankel(total):
    parts = []
    for b in range(3):
        row = jnp.concatenate([total[:, b * T : (b + 1) * T], jnp.zeros((1, T), F32)], axis=1)
        row = jnp.broadcast_to(row, (T, 2 * T))
        parts.append(pltpu.roll(row, T + 1, 1, stride=1, stride_axis=0)[:, :T])
    flipped = jnp.concatenate(parts, axis=1)
    flip = jnp.where(iota((T, T), 0) + iota((T, T), 1) == T - 1, 1.0, 0.0).astype(F32)
    lagged = jnp.dot(flip, flipped, precision=HIGHEST, preferred_element_type=F32)
    return jnp.concatenate([lagged[:, b * T : (b + 1) * T] for b in range(3)], axis=0)


def correlate(flux, lagged):
    out = jnp.dot(flux, lagged, precision=HIGHEST, preferred_element_type=F32)
    return out / (T - iota(out.shape, 1)).astype(F32)


class Group:
    def __init__(self, sems, index):
        self.send_sem, self.recv_sem = sems.at[0, index], sems.at[1, index]

    def describe(self, src, dst, device):
        return pltpu.make_async_remote_copy(
            src_ref=src, dst_ref=dst, send_sem=self.send_sem, recv_sem=self.recv_sem,
            device_id=device, device_id_type=MESH,
        )

    def put(self, src, dst, device):
        self.device = device
        self.describe(src, dst, device).start()

    def arrive(self, whole):
        self.whole = whole
        self.describe(whole, whole, self.device).wait_recv()

    def left(self):
        self.describe(self.whole, self.whole, self.device).wait_send()


def kernel(
    vel, vir, gho, eig, slots, counts, out,
    ev, ms, nv, rs, gh, ep, vp, part, cr, cs,
    rx, x1, ry, rr, rh, ryb, y1b, rxb, rhc, h1c, rxc, x1c, ryc,
    tp, tc, tx, ty, th, sz, sp,
    load_sem, sems, relay,
):
    a = lax.axis_index("atom")
    m = lax.axis_index("mode")
    c, x, h, y = lax.rem(a, 2), lax.rem(lax.div(a, 2), 4), lax.rem(lax.div(a, 8), 2), lax.div(a, 16)
    z = h * NM + m
    place = lax.rem(a, 8)

    def dev(y=y, h=h, x=x, c=c, m=m):
        return (((y * NH + h) * NX + x) * NC + c, m)

    core = dev(c=1 - c)
    h_peer = dev(h=1 - h)
    x_peers = [lax.rem(x + k, NX) for k in range(1, NX)]
    y_peers = [lax.rem(y + k, NY) for k in range(1, NY)]
    z_peers = [(lax.rem(z + i // 2, 8), lax.rem(c + i % 2, NC)) for i in range(1, 16)]
    p_peers = [(lax.rem(y + i // 4, NY), lax.rem(x + i % 4, NX)) for i in range(1, 32)]
    domains = NY * NH * NX * NC
    above = (lax.rem(a + 1, domains), jnp.where(place == 7, 3 - m, m))
    below = (lax.rem(a + domains - 1, domains), jnp.where(place == 0, 3 - m, m))
    near = [dev(x=x_peers[0]), dev(x=x_peers[2]), dev(y=y_peers[0]), dev(y=y_peers[6])]
    near += [dev(h=lax.div(zz, NM), m=lax.rem(zz, NM)) for zz in (lax.rem(z + 1, 8), lax.rem(z + 7, 8))]

    barrier = pltpu.get_barrier_semaphore()
    for device in [above, below] + near:
        pl.semaphore_signal(barrier, 1, device_id=device, device_id_type=MESH)
    loads = [
        pltpu.make_async_copy(counts, nv, load_sem.at[0]),
        pltpu.make_async_copy(vel, ms.at[:, 0:T], load_sem.at[1]),
        pltpu.make_async_copy(vir, ms.at[:, T:], load_sem.at[2]),
    ]
    loads += [
        pltpu.make_async_copy(eig.at[pl.ds(384 * i, 384)], ev.at[pl.ds(384 * i, 384)], load_sem.at[3 + i])
        for i in range(4)
    ]
    for load in loads:
        load.start()

    used = [0]

    def group():
        used[0] += 1
        return Group(sems, used[0] - 1)

    def tell(step):
        for device in near:
            pl.semaphore_signal(relay.at[step], 1, device_id=device, device_id_type=MESH)

    def told(step):
        pl.semaphore_wait(relay.at[step], len(near))

    pl.semaphore_wait(barrier, 2 + len(near))
    places = [group(), group()]
    places[0].put(slots, rs.at[0], above)
    places[1].put(slots, rs.at[1], below)
    ghost_copies = []
    for b in range(3):
        cols = pl.ds(b * T, T)
        for side, device in enumerate((above, below)):
            ghost_copies.append(group())
            ghost_copies[-1].put(gho.at[pl.ds(FACE * (1 - side), FACE), cols], gh.at[b, side], device)
    tell(0)

    for load in loads[:3]:
        load.wait()
    alive = jnp.where(iota((ms.shape[0], T), 0) < 3 * nv[0], 1.0, 0.0).astype(BF16)
    for q in range(4):
        ms[:, q * T : (q + 1) * T] = ms[:, q * T : (q + 1) * T] * alive

    for load in loads[3:]:
        load.wait()
    for j in range(4):
        acc = dot_rows(ev[:, 256 * j : 256 * (j + 1)], ms[...])
        for q in range(4):
            part[q, 2 * j : 2 * j + 2] = acc[:, q * T : (q + 1) * T].reshape(2, NH, NX, NC, K, T)
        if j == 1:
            told(0)
            tell(1)

    cores = []

    def core_send(b):
        cores.append(group())
        cores[-1].put(part.at[b, :, :, :, 1 - c], cr.at[b], core)

    def core_sum(b):
        cores[b].arrive(cr.at[b])
        cs[b] = part[b, :, :, :, c] + cr[b]

    def over_x(src, dst, cut):
        copies = group()
        for n, xx in enumerate(x_peers):
            copies.put(cut(src, xx), dst.at[n], dev(x=xx))
        return copies

    def over_y(src, dst):
        copies = group()
        for n, yy in enumerate(y_peers):
            copies.put(src.at[yy], dst.at[n], dev(y=yy))
        return copies

    def over_h(src, dst):
        copies = group()
        copies.put(src, dst, h_peer)
        return copies

    def gather(copies, own, slots_of):
        copies.arrive(slots_of)
        for n in range(slots_of.shape[0]):
            own = own + slots_of[n]
        return own

    core_send(0)
    told(1)
    tell(2)

    total = dot_rows(ms[:, :T], ms[:, T:])
    for side in range(2):
        places[side].arrive(rs.at[side])
        rows = pl.ds(FACE * side, FACE)
        put = placing(rs[side], side)
        ep[rows, :] = dot_rows(put, ev[rows, :]).astype(BF16)
        vp[rows, :] = dot_rows(put, ms[rows, 0:T]).astype(BF16)
    core_sum(0)
    xs0 = over_x(cs.at[0], rx.at[0], lambda ref, xx: ref.at[:, :, xx])
    told(2)

    def add_ghosts(b):
        for side in range(2):
            ghost_copies[2 * (b - 1) + side].arrive(gh.at[b - 1, side])
        ghosts = gh[b - 1].reshape(2 * FACE, T)
        for j in range(4):
            now = dot_rows(ep[:, 256 * j : 256 * (j + 1)], ghosts).reshape(2, NH, NX, NC, K, T)
            part[b, 2 * j : 2 * j + 2] = part[b, 2 * j : 2 * j + 2] + now
        core_send(b)

    add_ghosts(1)
    add_ghosts(2)
    core_sum(1)
    ysb = over_y(cs.at[1], ryb)
    add_ghosts(3)
    core_sum(2)
    xs2 = over_x(cs.at[2], rx.at[1], lambda ref, xx: ref.at[:, :, xx])

    diagonal = iota((T, T), 0) == iota((T, T), 1)
    parts = []
    for b in range(3):
        now = total[:, b * T : (b + 1) * T] + dot_rows(vp[...], gh[b].reshape(2 * FACE, T))
        parts.append(jnp.sum(jnp.where(diagonal, now, 0.0), axis=0, keepdims=True))
    core_sum(3)
    hsc = over_h(cs.at[3, :, 1 - h], rhc)
    tp[...] = jnp.concatenate(parts, axis=1)
    tot_core = group()
    tot_core.put(tp, tc, core)

    x1[0] = gather(xs0, cs[0, :, :, x], rx.at[0])
    ys0 = over_y(x1.at[0], ry.at[0])
    tot_core.arrive(tc)
    tx[x] = tp[...] + tc[...]
    tot_x = group()
    for xx in x_peers:
        tot_x.put(tx.at[x], tx.at[x], dev(x=xx))
    x1[1] = gather(xs2, cs[2, :, :, x], rx.at[1])
    ys2 = over_y(x1.at[1], ry.at[1])
    hsc.arrive(rhc)
    h1c[...] = cs[3, :, h] + rhc[...]
    xsc = over_x(h1c, rxc, lambda ref, xx: ref.at[:, xx])
    tot_x.arrive(tx.at[pl.ds(0, 3)])
    ty[y] = ((tx[0] + tx[1]) + tx[2]) + tx[3]
    tot_y = group()
    for yy in y_peers:
        tot_y.put(ty.at[y], ty.at[y], dev(y=yy))
    y1b[...] = gather(ysb, cs[1, y], ryb)
    xsb = over_x(y1b, rxb, lambda ref, xx: ref.at[:, xx])
    x1c[...] = gather(xsc, h1c[:, x], rxc)
    ysc = over_y(x1c, ryc)
    rr[0] = gather(ys0, x1[0, y], ry.at[0])
    hs0 = over_h(rr.at[0, 1 - h], rh.at[0])
    tot_y.arrive(ty.at[pl.ds(0, 7)])
    summed = ty[0]
    for n in range(1, NY):
        summed = summed + ty[n]
    th[0] = summed
    tot_h = over_h(th.at[0], th.at[1])
    rr[2] = gather(ys2, x1[1, y], ry.at[1])
    hs2 = over_h(rr.at[2, 1 - h], rh.at[2])
    rr[1] = gather(xsb, y1b[:, x], rxb)
    hs1 = over_h(rr.at[1, 1 - h], rh.at[1])
    tot_h.arrive(th.at[1])
    lagged = hankel((th[0] + th[1]) * (1.0 / math.sqrt(ms.shape[0] // 3 * domains)))
    last = gather(ysc, x1c[y], ryc)
    hs0.arrive(rh.at[0])
    hs2.arrive(rh.at[2])
    hs1.arrive(rh.at[1])
    final = [rr[b, h] + rh[b] for b in range(3)] + [last]
    flux = jnp.concatenate([final[0] * final[1 + b] for b in range(3)], axis=1)

    here = z * NC + c
    sz[here] = jnp.sum(flux, axis=0, keepdims=True)
    szs = group()
    for zz, cc in z_peers:
        szs.put(sz.at[here], sz.at[here], dev(h=lax.div(zz, NM), m=lax.rem(zz, NM), c=cc))
    for b in range(3):
        out[b] = flux[:, b * T : (b + 1) * T]
    out[3] = correlate(flux, lagged)
    for copies in places + ghost_copies + cores:
        copies.left()
    for copies in (xs0, ys0, hs0, ysb, xsb, hs1, xs2, ys2, hs2, hsc, xsc, ysc):
        copies.left()
    for copies in (tot_core, tot_x, tot_y, tot_h):
        copies.left()
    szs.arrive(sz.at[pl.ds(0, 15)])
    summed = sz[0]
    for n in range(1, 16):
        summed = summed + sz[n]
    there = y * NX + x
    sp[there] = summed
    sps = group()
    for yy, xx in p_peers:
        sps.put(sp.at[there], sp.at[there], dev(y=yy, x=xx))
    szs.left()
    sps.arrive(sp.at[pl.ds(0, 31)])
    slab = sp[0]
    for n in range(1, 32):
        slab = slab + sp[n]
    out[4] = correlate(jnp.broadcast_to(slab, (8, 3 * T)), lagged) * (1.0 / math.sqrt(NM * domains * K))
    sps.left()


def deliver(held, flux, corr, slab):
    flux[0] = held[0:3]
    corr[0] = held[3, :, :LAGS]
    slab[...] = held[4, 0:1, :LAGS]


def per_device(velocity, local_virial, ghost_virial, eigvec, ghost_slot, counts):
    rows, modes = eigvec.shape
    vmem = pltpu.VMEM
    dma = pltpu.SemaphoreType.DMA
    scratch = [
        vmem((rows, modes), BF16),
        vmem((rows, 4 * T), BF16),
        pltpu.SMEM((1,), jnp.int32),
        vmem((2, 1, T), jnp.int32),
        vmem((3, 2, FACE, T), BF16),
        vmem((2 * FACE, modes), BF16),
        vmem((2 * FACE, T), BF16),
        vmem((4, NY, NH, NX, NC, K, T), F32),
        vmem((4, NY, NH, NX, K, T), F32),
        vmem((4, NY, NH, NX, K, T), F32),
        vmem((2, 3, NY, NH, K, T), F32),
        vmem((2, NY, NH, K, T), F32),
        vmem((2, NY - 1, NH, K, T), F32),
        vmem((3, NH, K, T), F32),
        vmem((3, K, T), F32),
        vmem((NY - 1, NH, NX, K, T), F32),
        vmem((NH, NX, K, T), F32),
        vmem((3, NH, K, T), F32),
        vmem((NY, NX, K, T), F32),
        vmem((NY, NX, K, T), F32),
        vmem((3, NY, K, T), F32),
        vmem((NY, K, T), F32),
        vmem((NY - 1, K, T), F32),
        vmem((1, 3 * T), F32),
        vmem((1, 3 * T), F32),
        vmem((NX, 1, 3 * T), F32),
        vmem((NY, 1, 3 * T), F32),
        vmem((2, 1, 3 * T), F32),
        vmem((16, 1, 3 * T), F32),
        vmem((32, 1, 3 * T), F32),
        dma((7,)),
        dma((2, 32)),
        pltpu.SemaphoreType.REGULAR((3,)),
    ]
    held = pl.pallas_call(
        kernel,
        out_shape=jax.ShapeDtypeStruct((5, K, T), F32),
        in_specs=[pl.BlockSpec(memory_space=pltpu.HBM)] * 6,
        out_specs=pl.BlockSpec(memory_space=vmem),
        scratch_shapes=scratch,
        compiler_params=pltpu.CompilerParams(
            collective_id=0, has_side_effects=True, vmem_limit_bytes=56 * 2**20
        ),
        name="green_kubo",
    )(velocity, local_virial, ghost_virial, eigvec, ghost_slot.reshape(1, T), counts)
    flux, corr, slab = pl.pallas_call(
        deliver,
        out_shape=(
            jax.ShapeDtypeStruct((1, 3, K, T), F32),
            jax.ShapeDtypeStruct((1, K, LAGS), F32),
            jax.ShapeDtypeStruct((1, LAGS), F32),
        ),
        name="deliver",
    )(held)
    return jnp.transpose(flux, (0, 2, 1, 3)), corr, slab.reshape(LAGS)


def solution(mesh):
    return jax.shard_map(
        per_device,
        mesh=mesh,
        in_specs=(
            P("atom", None),
            P("atom", None),
            P("atom", None),
            P("atom", "mode"),
            P("atom"),
            P("atom"),
        ),
        out_specs=(P("mode", "atom", None, None), P("mode", "atom", None), P()),
        check_vma=False,
    )
```

```python
import functools
import math

import jax
import jax.numpy as jnp
from jax import lax
from jax.experimental import pallas as pl
from jax.experimental.pallas import tpu as pltpu
from jax.sharding import PartitionSpec as P

MESH = pl.DeviceIdType.MESH
F32 = jnp.float32
BF16 = jnp.bfloat16
HIGHEST = lax.Precision.HIGHEST
NY, NH, NX, NC, NM = 8, 2, 4, 2, 4
T = 128
K = 8
FACE = 192
LAGS = 64
RING = (4, 3, 5, 2, 6, 1, 7)


def dot_rows(left, right):
    return lax.dot_general(left, right, (((0,), (0,)), ((), ())), preferred_element_type=F32)


def iota(shape, dim):
    return lax.broadcasted_iota(jnp.int32, shape, dim)


def placing(slots, side):
    first = 64 * (1 - side)
    lowest = 64 * side
    ghost = iota((T, FACE), 0) - first
    third = lax.shift_right_logical(iota((T, FACE), 1) * 171, 9)
    spread = jnp.where(ghost == third, 1.0, 0.0).astype(BF16)
    slot = (slots - lowest).astype(F32).astype(BF16)
    slot = jnp.dot(jnp.broadcast_to(slot, (8, T)), spread, preferred_element_type=F32)
    lane = iota((8, FACE), 1)
    third = lax.shift_right_logical(lane * 171, 9)
    target = 3 * slot.astype(jnp.int32) + (lane - 3 * third)
    return jnp.where(iota((FACE, FACE), 0) == target[0:1, :], 1.0, 0.0).astype(BF16)


def hankel(total):
    parts = []
    for b in range(3):
        row = jnp.concatenate([total[:, b * T : (b + 1) * T], jnp.zeros((1, T), F32)], axis=1)
        row = jnp.broadcast_to(row, (T, 2 * T))
        parts.append(pltpu.roll(row, T + 1, 1, stride=1, stride_axis=0)[:, :T])
    flipped = jnp.concatenate(parts, axis=1)
    flip = jnp.where(iota((T, T), 0) + iota((T, T), 1) == T - 1, 1.0, 0.0).astype(F32)
    lagged = jnp.dot(flip, flipped, precision=HIGHEST, preferred_element_type=F32)
    return jnp.concatenate([lagged[:, b * T : (b + 1) * T] for b in range(3)], axis=0)


def correlate(flux, lagged):
    out = jnp.dot(flux, lagged, precision=HIGHEST, preferred_element_type=F32)
    return out / (T - iota(out.shape, 1)).astype(F32)


class Group:
    def __init__(self, sems, index):
        self.send_sem, self.recv_sem = sems.at[0, index], sems.at[1, index]

    def describe(self, src, dst, device):
        return pltpu.make_async_remote_copy(
            src_ref=src, dst_ref=dst, send_sem=self.send_sem, recv_sem=self.recv_sem,
            device_id=device, device_id_type=MESH,
        )

    def put(self, src, dst, device):
        self.device = device
        self.describe(src, dst, device).start()

    def arrive(self, whole):
        self.whole = whole
        self.describe(whole, whole, self.device).wait_recv()

    def left(self):
        self.describe(self.whole, self.whole, self.device).wait_send()


def kernel(
    vel, vir, gho, eig, slots, counts, out,
    ev, ms, nv, rs, gh, ep, vp, part, cr, cs,
    rx, x1, ry, rr, rh, ryb, y1b, rxb, rhc, h1c, rxc, x1c, ryc,
    tp, tc, tx, ty, th, sz, sp,
    load_sem, sems, relay,
):
    a = lax.axis_index("atom")
    m = lax.axis_index("mode")
    c, x, h, y = lax.rem(a, 2), lax.rem(lax.div(a, 2), 4), lax.rem(lax.div(a, 8), 2), lax.div(a, 16)
    z = h * NM + m
    place = lax.rem(a, 8)

    def dev(y=y, h=h, x=x, c=c, m=m):
        return (((y * NH + h) * NX + x) * NC + c, m)

    core = dev(c=1 - c)
    h_peer = dev(h=1 - h)
    x_peers = [lax.rem(x + k, NX) for k in (2, 1, 3)]
    y_peers = [lax.rem(y + k, NY) for k in RING]
    z_peers = [(lax.rem(z + k, 8), lax.rem(c + i, NC)) for k in RING for i in (1, 0)] + [(z, 1 - c)]
    steps = sorted(range(1, 32), key=lambda i: -min(i // 4, NY - i // 4) - min(i % 4, NX - i % 4))
    p_peers = [(lax.rem(y + i // 4, NY), lax.rem(x + i % 4, NX)) for i in steps]
    domains = NY * NH * NX * NC
    above = (lax.rem(a + 1, domains), jnp.where(place == 7, 3 - m, m))
    below = (lax.rem(a + domains - 1, domains), jnp.where(place == 0, 3 - m, m))
    near = [dev(x=lax.rem(x + k, NX)) for k in (1, 3)] + [dev(y=lax.rem(y + k, NY)) for k in (1, 7)]
    near += [dev(h=lax.div(zz, NM), m=lax.rem(zz, NM)) for zz in (lax.rem(z + 1, 8), lax.rem(z + 7, 8))]

    barrier = pltpu.get_barrier_semaphore()
    for device in [above, below] + near:
        pl.semaphore_signal(barrier, 1, device_id=device, device_id_type=MESH)
    loads = [
        pltpu.make_async_copy(counts, nv, load_sem.at[0]),
        pltpu.make_async_copy(vel, ms.at[:, 0:T], load_sem.at[1]),
        pltpu.make_async_copy(vir, ms.at[:, T:], load_sem.at[2]),
    ]
    loads += [
        pltpu.make_async_copy(eig.at[pl.ds(384 * i, 384)], ev.at[pl.ds(384 * i, 384)], load_sem.at[3 + i])
        for i in range(4)
    ]
    for load in loads:
        load.start()

    used = [0]

    def group():
        used[0] += 1
        return Group(sems, used[0] - 1)

    def tell(step):
        for device in near:
            pl.semaphore_signal(relay.at[step], 1, device_id=device, device_id_type=MESH)

    def told(step):
        pl.semaphore_wait(relay.at[step], len(near))

    pl.semaphore_wait(barrier, 2 + len(near))
    places = [group(), group()]
    places[0].put(slots, rs.at[0], above)
    places[1].put(slots, rs.at[1], below)
    ghost_copies = {}
    for b in (2, 0, 1):
        cols = pl.ds(b * T, T)
        for side, device in enumerate((above, below)):
            ghost_copies[b, side] = group()
            ghost_copies[b, side].put(gho.at[pl.ds(FACE * (1 - side), FACE), cols], gh.at[b, side], device)
    tell(0)

    for load in loads[:3]:
        load.wait()
    alive = jnp.where(iota((ms.shape[0], T), 0) < 3 * nv[0], 1.0, 0.0).astype(BF16)
    for q in range(4):
        ms[:, q * T : (q + 1) * T] = ms[:, q * T : (q + 1) * T] * alive

    for load in loads[3:]:
        load.wait()
    for j in range(4):
        acc = dot_rows(ev[:, 256 * j : 256 * (j + 1)], ms[...])
        for q in range(4):
            part[q, 2 * j : 2 * j + 2] = acc[:, q * T : (q + 1) * T].reshape(2, NH, NX, NC, K, T)
        if j == 1:
            told(0)
            tell(1)

    cores = {}

    def core_send(b):
        cores[b] = group()
        cores[b].put(part.at[b, :, :, :, 1 - c], cr.at[b], core)

    def core_sum(b):
        cores[b].arrive(cr.at[b])
        cs[b] = part[b, :, :, :, c] + cr[b]

    def over_x(src, dst, cut):
        copies = group()
        for n, xx in enumerate(x_peers):
            copies.put(cut(src, xx), dst.at[n], dev(x=xx))
        return copies

    def over_y(src, dst):
        copies = group()
        for n, yy in enumerate(y_peers):
            copies.put(src.at[yy], dst.at[n], dev(y=yy))
        return copies

    def over_h(src, dst):
        copies = group()
        copies.put(src, dst, h_peer)
        return copies

    def gather(copies, own, slots_of):
        copies.arrive(slots_of)
        for n in range(slots_of.shape[0]):
            own = own + slots_of[n]
        return own

    core_send(0)
    told(1)
    tell(2)

    for side in range(2):
        places[side].arrive(rs.at[side])
        rows = pl.ds(FACE * side, FACE)
        put = placing(rs[side], side)
        ep[rows, :] = dot_rows(put, ev[rows, :]).astype(BF16)
        vp[rows, :] = dot_rows(put, ms[rows, 0:T]).astype(BF16)
    core_sum(0)
    xs0 = over_x(cs.at[0], rx.at[0], lambda ref, xx: ref.at[:, :, xx])
    told(2)

    def add_ghosts(b):
        for side in range(2):
            ghost_copies[b - 1, side].arrive(gh.at[b - 1, side])
        ghosts = gh[b - 1].reshape(2 * FACE, T)
        for j in range(4):
            now = dot_rows(ep[:, 256 * j : 256 * (j + 1)], ghosts).reshape(2, NH, NX, NC, K, T)
            part[b, 2 * j : 2 * j + 2] = part[b, 2 * j : 2 * j + 2] + now
        core_send(b)

    add_ghosts(3)
    add_ghosts(1)
    core_sum(3)
    hsc = over_h(cs.at[3, :, 1 - h], rhc)
    add_ghosts(2)
    core_sum(1)
    ysb = over_y(cs.at[1], ryb)
    core_sum(2)
    xs2 = over_x(cs.at[2], rx.at[1], lambda ref, xx: ref.at[:, :, xx])

    total = dot_rows(ms[:, :T], ms[:, T:])
    diagonal = iota((T, T), 0) == iota((T, T), 1)
    parts = []
    for b in range(3):
        now = total[:, b * T : (b + 1) * T] + dot_rows(vp[...], gh[b].reshape(2 * FACE, T))
        parts.append(jnp.sum(jnp.where(diagonal, now, 0.0), axis=0, keepdims=True))
    tp[...] = jnp.concatenate(parts, axis=1)
    tot_core = group()
    tot_core.put(tp, tc, core)

    x1[0] = gather(xs0, cs[0, :, :, x], rx.at[0])
    ys0 = over_y(x1.at[0], ry.at[0])
    tot_core.arrive(tc)
    tx[x] = tp[...] + tc[...]
    tot_x = group()
    for xx in x_peers:
        tot_x.put(tx.at[x], tx.at[x], dev(x=xx))
    hsc.arrive(rhc)
    h1c[...] = cs[3, :, h] + rhc[...]
    xsc = over_x(h1c, rxc, lambda ref, xx: ref.at[:, xx])
    x1[1] = gather(xs2, cs[2, :, :, x], rx.at[1])
    ys2 = over_y(x1.at[1], ry.at[1])
    tot_x.arrive(tx.at[pl.ds(0, 3)])
    ty[y] = ((tx[0] + tx[1]) + tx[2]) + tx[3]
    tot_y = group()
    for yy in y_peers:
        tot_y.put(ty.at[y], ty.at[y], dev(y=yy))
    y1b[...] = gather(ysb, cs[1, y], ryb)
    xsb = over_x(y1b, rxb, lambda ref, xx: ref.at[:, xx])
    x1c[...] = gather(xsc, h1c[:, x], rxc)
    ysc = over_y(x1c, ryc)
    rr[0] = gather(ys0, x1[0, y], ry.at[0])
    hs0 = over_h(rr.at[0, 1 - h], rh.at[0])
    tot_y.arrive(ty.at[pl.ds(0, 7)])
    summed = ty[0]
    for n in range(1, NY):
        summed = summed + ty[n]
    th[0] = summed
    tot_h = over_h(th.at[0], th.at[1])
    rr[2] = gather(ys2, x1[1, y], ry.at[1])
    hs2 = over_h(rr.at[2, 1 - h], rh.at[2])
    rr[1] = gather(xsb, y1b[:, x], rxb)
    hs1 = over_h(rr.at[1, 1 - h], rh.at[1])
    tot_h.arrive(th.at[1])
    lagged = hankel((th[0] + th[1]) * (1.0 / math.sqrt(ms.shape[0] // 3 * domains)))
    last = gather(ysc, x1c[y], ryc)
    hs0.arrive(rh.at[0])
    hs2.arrive(rh.at[2])
    hs1.arrive(rh.at[1])
    final = [rr[b, h] + rh[b] for b in range(3)] + [last]
    flux = jnp.concatenate([final[0] * final[1 + b] for b in range(3)], axis=1)

    here = z * NC + c
    sz[here] = jnp.sum(flux, axis=0, keepdims=True)
    szs = group()
    for zz, cc in z_peers:
        szs.put(sz.at[here], sz.at[here], dev(h=lax.div(zz, NM), m=lax.rem(zz, NM), c=cc))
    for b in range(3):
        out[b] = flux[:, b * T : (b + 1) * T]
    out[3] = correlate(flux, lagged)
    for copies in places + list(ghost_copies.values()) + list(cores.values()):
        copies.left()
    for copies in (xs0, ys0, hs0, ysb, xsb, hs1, xs2, ys2, hs2, hsc, xsc, ysc):
        copies.left()
    for copies in (tot_core, tot_x, tot_y, tot_h):
        copies.left()
    szs.arrive(sz.at[pl.ds(0, 15)])
    summed = sz[0]
    for n in range(1, 16):
        summed = summed + sz[n]
    there = y * NX + x
    sp[there] = summed
    sps = group()
    for yy, xx in p_peers:
        sps.put(sp.at[there], sp.at[there], dev(y=yy, x=xx))
    szs.left()
    sps.arrive(sp.at[pl.ds(0, 31)])
    slab = sp[0]
    for n in range(1, 32):
        slab = slab + sp[n]
    out[4] = correlate(jnp.broadcast_to(slab, (8, 3 * T)), lagged) * (1.0 / math.sqrt(NM * domains * K))
    sps.left()


def deliver(held, flux, corr, slab):
    flux[0] = held[0:3]
    corr[0] = held[3, :, :LAGS]
    slab[...] = held[4, 0:1, :LAGS]


def per_device(velocity, local_virial, ghost_virial, eigvec, ghost_slot, counts):
    rows, modes = eigvec.shape
    vmem = pltpu.VMEM
    dma = pltpu.SemaphoreType.DMA
    scratch = [
        vmem((rows, modes), BF16),
        vmem((rows, 4 * T), BF16),
        pltpu.SMEM((1,), jnp.int32),
        vmem((2, 1, T), jnp.int32),
        vmem((3, 2, FACE, T), BF16),
        vmem((2 * FACE, modes), BF16),
        vmem((2 * FACE, T), BF16),
        vmem((4, NY, NH, NX, NC, K, T), F32),
        vmem((4, NY, NH, NX, K, T), F32),
        vmem((4, NY, NH, NX, K, T), F32),
        vmem((2, 3, NY, NH, K, T), F32),
        vmem((2, NY, NH, K, T), F32),
        vmem((2, NY - 1, NH, K, T), F32),
        vmem((3, NH, K, T), F32),
        vmem((3, K, T), F32),
        vmem((NY - 1, NH, NX, K, T), F32),
        vmem((NH, NX, K, T), F32),
        vmem((3, NH, K, T), F32),
        vmem((NY, NX, K, T), F32),
        vmem((NY, NX, K, T), F32),
        vmem((3, NY, K, T), F32),
        vmem((NY, K, T), F32),
        vmem((NY - 1, K, T), F32),
        vmem((1, 3 * T), F32),
        vmem((1, 3 * T), F32),
        vmem((NX, 1, 3 * T), F32),
        vmem((NY, 1, 3 * T), F32),
        vmem((2, 1, 3 * T), F32),
        vmem((16, 1, 3 * T), F32),
        vmem((32, 1, 3 * T), F32),
        dma((7,)),
        dma((2, 32)),
        pltpu.SemaphoreType.REGULAR((3,)),
    ]
    held = pl.pallas_call(
        kernel,
        out_shape=jax.ShapeDtypeStruct((5, K, T), F32),
        in_specs=[pl.BlockSpec(memory_space=pltpu.HBM)] * 6,
        out_specs=pl.BlockSpec(memory_space=vmem),
        scratch_shapes=scratch,
        compiler_params=pltpu.CompilerParams(
            collective_id=0, has_side_effects=True, vmem_limit_bytes=56 * 2**20
        ),
        name="green_kubo",
    )(velocity, local_virial, ghost_virial, eigvec, ghost_slot.reshape(1, T), counts)
    flux, corr, slab = pl.pallas_call(
        deliver,
        out_shape=(
            jax.ShapeDtypeStruct((1, 3, K, T), F32),
            jax.ShapeDtypeStruct((1, K, LAGS), F32),
            jax.ShapeDtypeStruct((1, LAGS), F32),
        ),
        name="deliver",
    )(held)
    return jnp.transpose(flux, (0, 2, 1, 3)), corr, slab.reshape(LAGS)


def solution(mesh):
    return jax.shard_map(
        per_device,
        mesh=mesh,
        in_specs=(
            P("atom", None),
            P("atom", None),
            P("atom", None),
            P("atom", "mode"),
            P("atom"),
            P("atom"),
        ),
        out_specs=(P("mode", "atom", None, None), P("mode", "atom", None), P()),
        check_vma=False,
    )
```

```python
import functools
import math

import jax
import jax.numpy as jnp
from jax import lax
from jax.experimental import pallas as pl
from jax.experimental.pallas import tpu as pltpu
from jax.sharding import PartitionSpec as P

MESH = pl.DeviceIdType.MESH
F32 = jnp.float32
BF16 = jnp.bfloat16
I16 = jnp.int16
TOP = 32767.0
HIGHEST = lax.Precision.HIGHEST
NY, NH, NX, NC, NM = 8, 2, 4, 2, 4
T = 128
K = 8
FACE = 192
LAGS = 64
RING = (4, 3, 5, 2, 6, 1, 7)


def dot_rows(left, right):
    return lax.dot_general(left, right, (((0,), (0,)), ((), ())), preferred_element_type=F32)


def iota(shape, dim):
    return lax.broadcasted_iota(jnp.int32, shape, dim)


def placing(slots, side):
    first = 64 * (1 - side)
    lowest = 64 * side
    ghost = iota((T, FACE), 0) - first
    third = lax.shift_right_logical(iota((T, FACE), 1) * 171, 9)
    spread = jnp.where(ghost == third, 1.0, 0.0).astype(BF16)
    slot = (slots - lowest).astype(F32).astype(BF16)
    slot = jnp.dot(jnp.broadcast_to(slot, (8, T)), spread, preferred_element_type=F32)
    lane = iota((8, FACE), 1)
    third = lax.shift_right_logical(lane * 171, 9)
    target = 3 * slot.astype(jnp.int32) + (lane - 3 * third)
    return jnp.where(iota((FACE, FACE), 0) == target[0:1, :], 1.0, 0.0).astype(BF16)


def scale_of(rows):
    top = jnp.max(jnp.abs(rows), axis=0, keepdims=True)
    step = jnp.maximum(top, 1e-30) * (1.0 / TOP)
    e = jnp.floor(jnp.log2(step)) - 13.0
    return e, jnp.minimum(jnp.ceil(step * jnp.exp2(-e)), TOP)


def code(rows, scale):
    e, f = scale
    scaled = jnp.clip(jnp.round(rows * (jnp.exp2(-e) / f)), -TOP, TOP)
    return scaled.astype(jnp.int32).astype(I16)


def code_of(scale):
    e, f = (jnp.broadcast_to(part, (8, T)) for part in scale)
    return jnp.concatenate([e, f], axis=0).astype(jnp.int32).astype(I16)


def decode(coded):
    count = coded.shape[0] - 16
    scale = coded[count:].astype(jnp.int32).astype(F32)
    return coded[:count].astype(jnp.int32).astype(F32) * (jnp.exp2(scale[0:1]) * scale[8:9])


def hankel(total):
    parts = []
    for b in range(3):
        row = jnp.concatenate([total[:, b * T : (b + 1) * T], jnp.zeros((1, T), F32)], axis=1)
        row = jnp.broadcast_to(row, (T, 2 * T))
        parts.append(pltpu.roll(row, T + 1, 1, stride=1, stride_axis=0)[:, :T])
    flipped = jnp.concatenate(parts, axis=1)
    flip = jnp.where(iota((T, T), 0) + iota((T, T), 1) == T - 1, 1.0, 0.0).astype(F32)
    lagged = jnp.dot(flip, flipped, precision=HIGHEST, preferred_element_type=F32)
    return jnp.concatenate([lagged[:, b * T : (b + 1) * T] for b in range(3)], axis=0)


def correlate(flux, lagged):
    out = jnp.dot(flux, lagged, precision=HIGHEST, preferred_element_type=F32)
    return out / (T - iota(out.shape, 1)).astype(F32)


class Group:
    def __init__(self, sems, index):
        self.send_sem, self.recv_sem = sems.at[0, index], sems.at[1, index]

    def describe(self, src, dst, device):
        return pltpu.make_async_remote_copy(
            src_ref=src, dst_ref=dst, send_sem=self.send_sem, recv_sem=self.recv_sem,
            device_id=device, device_id_type=MESH,
        )

    def put(self, src, dst, device):
        self.device = device
        self.describe(src, dst, device).start()

    def arrive(self, whole):
        self.whole = whole
        self.describe(whole, whole, self.device).wait_recv()

    def left(self):
        self.describe(self.whole, self.whole, self.device).wait_send()


def kernel(
    vel, vir, gho, eig, slots, counts, out,
    ev, ms, nv, rs, gh, ep, vp, part, cr, cs, qx, qy, qh,
    rx, x1, ry, rr, rh, ryb, y1b, rxb, rhc, h1c, rxc, x1c, ryc,
    tp, tc, tx, ty, th, sz, sp,
    load_sem, sems, relay,
):
    a = lax.axis_index("atom")
    m = lax.axis_index("mode")
    c, x, h, y = lax.rem(a, 2), lax.rem(lax.div(a, 2), 4), lax.rem(lax.div(a, 8), 2), lax.div(a, 16)
    z = h * NM + m
    place = lax.rem(a, 8)

    def dev(y=y, h=h, x=x, c=c, m=m):
        return (((y * NH + h) * NX + x) * NC + c, m)

    core = dev(c=1 - c)
    h_peer = dev(h=1 - h)
    x_peers = [lax.rem(x + k, NX) for k in (2, 1, 3)]
    y_peers = [lax.rem(y + k, NY) for k in RING]
    z_peers = [(lax.rem(z + k, 8), lax.rem(c + i, NC)) for k in RING for i in (1, 0)] + [(z, 1 - c)]
    steps = sorted(range(1, 32), key=lambda i: -min(i // 4, NY - i // 4) - min(i % 4, NX - i % 4))
    p_peers = [(lax.rem(y + i // 4, NY), lax.rem(x + i % 4, NX)) for i in steps]
    domains = NY * NH * NX * NC
    above = (lax.rem(a + 1, domains), jnp.where(place == 7, 3 - m, m))
    below = (lax.rem(a + domains - 1, domains), jnp.where(place == 0, 3 - m, m))
    near = [dev(x=lax.rem(x + k, NX)) for k in (1, 3)] + [dev(y=lax.rem(y + k, NY)) for k in (1, 7)]
    near += [dev(h=lax.div(zz, NM), m=lax.rem(zz, NM)) for zz in (lax.rem(z + 1, 8), lax.rem(z + 7, 8))]

    barrier = pltpu.get_barrier_semaphore()
    for device in [above, below] + near:
        pl.semaphore_signal(barrier, 1, device_id=device, device_id_type=MESH)
    loads = [
        pltpu.make_async_copy(counts, nv, load_sem.at[0]),
        pltpu.make_async_copy(vel, ms.at[:, 0:T], load_sem.at[1]),
        pltpu.make_async_copy(vir, ms.at[:, T:], load_sem.at[2]),
    ]
    loads += [
        pltpu.make_async_copy(eig.at[pl.ds(384 * i, 384)], ev.at[pl.ds(384 * i, 384)], load_sem.at[3 + i])
        for i in range(4)
    ]
    for load in loads:
        load.start()

    used = [0]

    def group():
        used[0] += 1
        return Group(sems, used[0] - 1)

    def tell(step):
        for device in near:
            pl.semaphore_signal(relay.at[step], 1, device_id=device, device_id_type=MESH)

    def told(step):
        pl.semaphore_wait(relay.at[step], len(near))

    pl.semaphore_wait(barrier, 2 + len(near))
    places = [group(), group()]
    places[0].put(slots, rs.at[0], above)
    places[1].put(slots, rs.at[1], below)
    ghost_copies = {}
    for b in (2, 0, 1):
        cols = pl.ds(b * T, T)
        for side, device in enumerate((above, below)):
            ghost_copies[b, side] = group()
            ghost_copies[b, side].put(gho.at[pl.ds(FACE * (1 - side), FACE), cols], gh.at[b, side], device)
    tell(0)

    for load in loads[:3]:
        load.wait()
    alive = jnp.where(iota((ms.shape[0], T), 0) < 3 * nv[0], 1.0, 0.0).astype(BF16)
    for q in range(4):
        ms[:, q * T : (q + 1) * T] = ms[:, q * T : (q + 1) * T] * alive

    for load in loads[3:]:
        load.wait()
    for j in range(4):
        acc = dot_rows(ev[:, 256 * j : 256 * (j + 1)], ms[...])
        for q in range(4):
            part[q, 2 * j : 2 * j + 2] = acc[:, q * T : (q + 1) * T].reshape(2, NH, NX, NC, K, T)
        if j == 1:
            told(0)
            tell(1)

    cores = {}

    def core_send(b):
        cores[b] = group()
        cores[b].put(part.at[b, :, :, :, 1 - c], cr.at[b], core)

    def core_sum(b):
        cores[b].arrive(cr.at[b])
        cs[b] = part[b, :, :, :, c] + cr[b]

    def over_x(src, dst, cut):
        copies = group()
        for n, xx in enumerate(x_peers):
            copies.put(cut(src, xx), dst.at[n], dev(x=xx))
        return copies

    def over_y(src, dst):
        copies = group()
        for n, yy in enumerate(y_peers):
            copies.put(src.at[yy], dst.at[n], dev(y=yy))
        return copies

    def over_h(src, dst):
        copies = group()
        copies.put(src, dst, h_peer)
        return copies

    def gather(copies, own, slots_of):
        copies.arrive(slots_of)
        for n in range(slots_of.shape[0]):
            own = own + slots_of[n]
        return own

    def code_over_x(i):
        block = cs[2 * i]
        scale = scale_of(block.reshape(512, T))
        for xx in range(NX):
            qx[i, xx, 0:128] = code(block[:, :, xx].reshape(128, T), scale)
            qx[i, xx, 128:144] = code_of(scale)
        return over_x(qx.at[i], rx.at[i], lambda ref, xx: ref.at[xx])

    def code_over_y():
        block = cs[1].reshape(512, T)
        scale = scale_of(block)
        qy[:, 0:64] = code(block, scale).reshape(NY, 64, T)
        for yy in range(NY):
            qy[yy, 64:80] = code_of(scale)
        return over_y(qy, ryb)

    def code_over_h():
        block = cs[3, :, 1 - h].reshape(256, T)
        scale = scale_of(block)
        qh[0:256] = code(block, scale)
        qh[256:272] = code_of(scale)
        return over_h(qh, rhc)

    def gather_coded(copies, own, slots_of):
        copies.arrive(slots_of)
        for n in range(slots_of.shape[0]):
            own = own + decode(slots_of[n])
        return own

    core_send(0)
    told(1)
    tell(2)

    for side in range(2):
        places[side].arrive(rs.at[side])
        rows = pl.ds(FACE * side, FACE)
        put = placing(rs[side], side)
        ep[rows, :] = dot_rows(put, ev[rows, :]).astype(BF16)
        vp[rows, :] = dot_rows(put, ms[rows, 0:T]).astype(BF16)
    core_sum(0)
    xs0 = code_over_x(0)
    told(2)

    def add_ghosts(b):
        for side in range(2):
            ghost_copies[b - 1, side].arrive(gh.at[b - 1, side])
        ghosts = gh[b - 1].reshape(2 * FACE, T)
        for j in range(4):
            now = dot_rows(ep[:, 256 * j : 256 * (j + 1)], ghosts).reshape(2, NH, NX, NC, K, T)
            part[b, 2 * j : 2 * j + 2] = part[b, 2 * j : 2 * j + 2] + now
        core_send(b)

    add_ghosts(3)
    add_ghosts(1)
    core_sum(3)
    hsc = code_over_h()
    add_ghosts(2)
    core_sum(1)
    ysb = code_over_y()
    core_sum(2)
    xs2 = code_over_x(1)

    total = dot_rows(ms[:, :T], ms[:, T:])
    diagonal = iota((T, T), 0) == iota((T, T), 1)
    parts = []
    for b in range(3):
        now = total[:, b * T : (b + 1) * T] + dot_rows(vp[...], gh[b].reshape(2 * FACE, T))
        parts.append(jnp.sum(jnp.where(diagonal, now, 0.0), axis=0, keepdims=True))
    tp[...] = jnp.concatenate(parts, axis=1)
    tot_core = group()
    tot_core.put(tp, tc, core)

    x1[0] = gather_coded(xs0, cs[0, :, :, x].reshape(128, T), rx.at[0]).reshape(NY, NH, K, T)
    ys0 = over_y(x1.at[0], ry.at[0])
    tot_core.arrive(tc)
    tx[x] = tp[...] + tc[...]
    tot_x = group()
    for xx in x_peers:
        tot_x.put(tx.at[x], tx.at[x], dev(x=xx))
    hsc.arrive(rhc)
    h1c[...] = cs[3, :, h] + decode(rhc[...]).reshape(NY, NX, K, T)
    xsc = over_x(h1c, rxc, lambda ref, xx: ref.at[:, xx])
    x1[1] = gather_coded(xs2, cs[2, :, :, x].reshape(128, T), rx.at[1]).reshape(NY, NH, K, T)
    ys2 = over_y(x1.at[1], ry.at[1])
    tot_x.arrive(tx.at[pl.ds(0, 3)])
    ty[y] = ((tx[0] + tx[1]) + tx[2]) + tx[3]
    tot_y = group()
    for yy in y_peers:
        tot_y.put(ty.at[y], ty.at[y], dev(y=yy))
    y1b[...] = gather_coded(ysb, cs[1, y].reshape(64, T), ryb).reshape(NH, NX, K, T)
    xsb = over_x(y1b, rxb, lambda ref, xx: ref.at[:, xx])
    x1c[...] = gather(xsc, h1c[:, x], rxc)
    ysc = over_y(x1c, ryc)
    rr[0] = gather(ys0, x1[0, y], ry.at[0])
    hs0 = over_h(rr.at[0, 1 - h], rh.at[0])
    tot_y.arrive(ty.at[pl.ds(0, 7)])
    summed = ty[0]
    for n in range(1, NY):
        summed = summed + ty[n]
    th[0] = summed
    tot_h = over_h(th.at[0], th.at[1])
    rr[2] = gather(ys2, x1[1, y], ry.at[1])
    hs2 = over_h(rr.at[2, 1 - h], rh.at[2])
    rr[1] = gather(xsb, y1b[:, x], rxb)
    hs1 = over_h(rr.at[1, 1 - h], rh.at[1])
    last = gather(ysc, x1c[y], ryc)
    hs0.arrive(rh.at[0])
    hs2.arrive(rh.at[2])
    hs1.arrive(rh.at[1])
    final = [rr[b, h] + rh[b] for b in range(3)] + [last]
    flux = jnp.concatenate([final[0] * final[1 + b] for b in range(3)], axis=1)

    here = z * NC + c
    sz[here] = jnp.sum(flux, axis=0, keepdims=True)
    szs = group()
    for zz, cc in z_peers:
        szs.put(sz.at[here], sz.at[here], dev(h=lax.div(zz, NM), m=lax.rem(zz, NM), c=cc))
    tot_h.arrive(th.at[1])
    lagged = hankel((th[0] + th[1]) * (1.0 / math.sqrt(ms.shape[0] // 3 * domains)))
    for b in range(3):
        out[b] = flux[:, b * T : (b + 1) * T]
    out[3] = correlate(flux, lagged)
    for copies in places + list(ghost_copies.values()) + list(cores.values()):
        copies.left()
    for copies in (xs0, ys0, hs0, ysb, xsb, hs1, xs2, ys2, hs2, hsc, xsc, ysc):
        copies.left()
    for copies in (tot_core, tot_x, tot_y, tot_h):
        copies.left()
    szs.arrive(sz.at[pl.ds(0, 15)])
    summed = sz[0]
    for n in range(1, 16):
        summed = summed + sz[n]
    there = y * NX + x
    sp[there] = summed
    sps = group()
    for yy, xx in p_peers:
        sps.put(sp.at[there], sp.at[there], dev(y=yy, x=xx))
    szs.left()
    sps.arrive(sp.at[pl.ds(0, 31)])
    slab = sp[0]
    for n in range(1, 32):
        slab = slab + sp[n]
    out[4] = correlate(jnp.broadcast_to(slab, (8, 3 * T)), lagged) * (1.0 / math.sqrt(NM * domains * K))
    sps.left()


def deliver(held, flux, corr, slab):
    flux[0] = held[0:3]
    corr[0] = held[3, :, :LAGS]
    slab[...] = held[4, 0:1, :LAGS]


def per_device(velocity, local_virial, ghost_virial, eigvec, ghost_slot, counts):
    rows, modes = eigvec.shape
    vmem = pltpu.VMEM
    dma = pltpu.SemaphoreType.DMA
    scratch = [
        vmem((rows, modes), BF16),
        vmem((rows, 4 * T), BF16),
        pltpu.SMEM((1,), jnp.int32),
        vmem((2, 1, T), jnp.int32),
        vmem((3, 2, FACE, T), BF16),
        vmem((2 * FACE, modes), BF16),
        vmem((2 * FACE, T), BF16),
        vmem((4, NY, NH, NX, NC, K, T), F32),
        vmem((4, NY, NH, NX, K, T), F32),
        vmem((4, NY, NH, NX, K, T), F32),
        vmem((2, NX, 144, T), I16),
        vmem((NY, 80, T), I16),
        vmem((272, T), I16),
        vmem((2, 3, 144, T), I16),
        vmem((2, NY, NH, K, T), F32),
        vmem((2, NY - 1, NH, K, T), F32),
        vmem((3, NH, K, T), F32),
        vmem((3, K, T), F32),
        vmem((NY - 1, 80, T), I16),
        vmem((NH, NX, K, T), F32),
        vmem((3, NH, K, T), F32),
        vmem((272, T), I16),
        vmem((NY, NX, K, T), F32),
        vmem((3, NY, K, T), F32),
        vmem((NY, K, T), F32),
        vmem((NY - 1, K, T), F32),
        vmem((1, 3 * T), F32),
        vmem((1, 3 * T), F32),
        vmem((NX, 1, 3 * T), F32),
        vmem((NY, 1, 3 * T), F32),
        vmem((2, 1, 3 * T), F32),
        vmem((16, 1, 3 * T), F32),
        vmem((32, 1, 3 * T), F32),
        dma((7,)),
        dma((2, 32)),
        pltpu.SemaphoreType.REGULAR((3,)),
    ]
    held = pl.pallas_call(
        kernel,
        out_shape=jax.ShapeDtypeStruct((5, K, T), F32),
        in_specs=[pl.BlockSpec(memory_space=pltpu.HBM)] * 6,
        out_specs=pl.BlockSpec(memory_space=vmem),
        scratch_shapes=scratch,
        compiler_params=pltpu.CompilerParams(
            collective_id=0, has_side_effects=True, vmem_limit_bytes=56 * 2**20
        ),
        name="green_kubo",
    )(velocity, local_virial, ghost_virial, eigvec, ghost_slot.reshape(1, T), counts)
    flux, corr, slab = pl.pallas_call(
        deliver,
        out_shape=(
            jax.ShapeDtypeStruct((1, 3, K, T), F32),
            jax.ShapeDtypeStruct((1, K, LAGS), F32),
            jax.ShapeDtypeStruct((1, LAGS), F32),
        ),
        name="deliver",
    )(held)
    return jnp.transpose(flux, (0, 2, 1, 3)), corr, slab.reshape(LAGS)


def solution(mesh):
    return jax.shard_map(
        per_device,
        mesh=mesh,
        in_specs=(
            P("atom", None),
            P("atom", None),
            P("atom", None),
            P("atom", "mode"),
            P("atom"),
            P("atom"),
        ),
        out_specs=(P("mode", "atom", None, None), P("mode", "atom", None), P()),
        check_vma=False,
    )
```

```python
import functools
import math

import jax
import jax.numpy as jnp
from jax import lax
from jax.experimental import pallas as pl
from jax.experimental.pallas import tpu as pltpu
from jax.sharding import PartitionSpec as P

MESH = pl.DeviceIdType.MESH
F32 = jnp.float32
BF16 = jnp.bfloat16
I16 = jnp.int16
TOP = 32767.0
HIGHEST = lax.Precision.HIGHEST
NY, NH, NX, NC, NM = 8, 2, 4, 2, 4
T = 128
K = 8
FACE = 192
LAGS = 64
RING = (4, 3, 5, 2, 6, 1, 7)
HX = ((1, 2), (1, 1), (1, 3), (1, 0), (0, 2), (0, 1), (0, 3))


def dot_rows(left, right):
    return lax.dot_general(left, right, (((0,), (0,)), ((), ())), preferred_element_type=F32)


def iota(shape, dim):
    return lax.broadcasted_iota(jnp.int32, shape, dim)


def placing(slots, side):
    first = 64 * (1 - side)
    lowest = 64 * side
    ghost = iota((T, FACE), 0) - first
    third = lax.shift_right_logical(iota((T, FACE), 1) * 171, 9)
    spread = jnp.where(ghost == third, 1.0, 0.0).astype(BF16)
    slot = (slots - lowest).astype(F32).astype(BF16)
    slot = jnp.dot(jnp.broadcast_to(slot, (8, T)), spread, preferred_element_type=F32)
    lane = iota((8, FACE), 1)
    third = lax.shift_right_logical(lane * 171, 9)
    target = 3 * slot.astype(jnp.int32) + (lane - 3 * third)
    return jnp.where(iota((FACE, FACE), 0) == target[0:1, :], 1.0, 0.0).astype(BF16)


def scale_of(rows):
    top = jnp.max(jnp.abs(rows), axis=0, keepdims=True)
    step = jnp.maximum(top, 1e-30) * (1.0 / TOP)
    e = jnp.floor(jnp.log2(step)) - 13.0
    return e, jnp.minimum(jnp.ceil(step * jnp.exp2(-e)), TOP)


def code(rows, scale):
    e, f = scale
    scaled = jnp.clip(jnp.round(rows * (jnp.exp2(-e) / f)), -TOP, TOP)
    return scaled.astype(jnp.int32).astype(I16)


def code_of(scale):
    e, f = (jnp.broadcast_to(part, (8, T)) for part in scale)
    return jnp.concatenate([e, f], axis=0).astype(jnp.int32).astype(I16)


def decode(coded):
    count = coded.shape[0] - 16
    scale = coded[count:].astype(jnp.int32).astype(F32)
    return coded[:count].astype(jnp.int32).astype(F32) * (jnp.exp2(scale[0:1]) * scale[8:9])


def hankel(total):
    parts = []
    for b in range(3):
        row = jnp.concatenate([total[:, b * T : (b + 1) * T], jnp.zeros((1, T), F32)], axis=1)
        row = jnp.broadcast_to(row, (T, 2 * T))
        parts.append(pltpu.roll(row, T + 1, 1, stride=1, stride_axis=0)[:, :T])
    flipped = jnp.concatenate(parts, axis=1)
    flip = jnp.where(iota((T, T), 0) + iota((T, T), 1) == T - 1, 1.0, 0.0).astype(F32)
    lagged = jnp.dot(flip, flipped, precision=HIGHEST, preferred_element_type=F32)
    return jnp.concatenate([lagged[:, b * T : (b + 1) * T] for b in range(3)], axis=0)


def correlate(flux, lagged):
    out = jnp.dot(flux, lagged, precision=HIGHEST, preferred_element_type=F32)
    return out / (T - iota(out.shape, 1)).astype(F32)


class Group:
    def __init__(self, sems, index):
        self.send_sem, self.recv_sem = sems.at[0, index], sems.at[1, index]

    def describe(self, src, dst, device):
        return pltpu.make_async_remote_copy(
            src_ref=src, dst_ref=dst, send_sem=self.send_sem, recv_sem=self.recv_sem,
            device_id=device, device_id_type=MESH,
        )

    def put(self, src, dst, device):
        self.device = device
        self.describe(src, dst, device).start()

    def arrive(self, whole):
        self.whole = whole
        self.describe(whole, whole, self.device).wait_recv()

    def left(self):
        self.describe(self.whole, self.whole, self.device).wait_send()


def kernel(
    vel, vir, gho, eig, slots, counts, out,
    ev, ms, nv, rs, gh, ep, vp, part, cr, cs, qx, qy, qh,
    rx, x1, ry, rr, rh, ryb, y1b, rxb, rhc, h1c, rxc, x1c, ryc,
    tp, tc, tx, ty, th, sz, sp,
    load_sem, sems, relay,
):
    a = lax.axis_index("atom")
    m = lax.axis_index("mode")
    c, x, h, y = lax.rem(a, 2), lax.rem(lax.div(a, 2), 4), lax.rem(lax.div(a, 8), 2), lax.div(a, 16)
    z = h * NM + m
    place = lax.rem(a, 8)

    def dev(y=y, h=h, x=x, c=c, m=m):
        return (((y * NH + h) * NX + x) * NC + c, m)

    core = dev(c=1 - c)
    h_peer = dev(h=1 - h)
    x_peers = [lax.rem(x + k, NX) for k in (2, 1, 3)]
    hx_peers = [(lax.rem(h + i, NH), lax.rem(x + k, NX)) for i, k in HX]
    y_peers = [lax.rem(y + k, NY) for k in RING]
    z_peers = [(lax.rem(z + k, 8), lax.rem(c + i, NC)) for k in RING for i in (1, 0)] + [(z, 1 - c)]
    steps = sorted(range(1, 32), key=lambda i: -min(i // 4, NY - i // 4) - min(i % 4, NX - i % 4))
    p_peers = [(lax.rem(y + i // 4, NY), lax.rem(x + i % 4, NX)) for i in steps]
    domains = NY * NH * NX * NC
    above = (lax.rem(a + 1, domains), jnp.where(place == 7, 3 - m, m))
    below = (lax.rem(a + domains - 1, domains), jnp.where(place == 0, 3 - m, m))
    near = [dev(x=lax.rem(x + k, NX)) for k in (1, 3)] + [dev(y=lax.rem(y + k, NY)) for k in (1, 7)]
    near += [dev(h=lax.div(zz, NM), m=lax.rem(zz, NM)) for zz in (lax.rem(z + 1, 8), lax.rem(z + 7, 8))]

    barrier = pltpu.get_barrier_semaphore()
    for device in [above, below] + near:
        pl.semaphore_signal(barrier, 1, device_id=device, device_id_type=MESH)
    loads = [
        pltpu.make_async_copy(counts, nv, load_sem.at[0]),
        pltpu.make_async_copy(vel, ms.at[:, 0:T], load_sem.at[1]),
        pltpu.make_async_copy(vir, ms.at[:, T:], load_sem.at[2]),
    ]
    loads += [
        pltpu.make_async_copy(eig.at[pl.ds(384 * i, 384)], ev.at[pl.ds(384 * i, 384)], load_sem.at[3 + i])
        for i in range(4)
    ]
    for load in loads:
        load.start()

    used = [0]

    def group():
        used[0] += 1
        return Group(sems, used[0] - 1)

    def tell(step):
        for device in near:
            pl.semaphore_signal(relay.at[step], 1, device_id=device, device_id_type=MESH)

    def told(step):
        pl.semaphore_wait(relay.at[step], len(near))

    pl.semaphore_wait(barrier, 2 + len(near))
    places = [group(), group()]
    places[0].put(slots, rs.at[0], above)
    places[1].put(slots, rs.at[1], below)
    ghost_copies = {}
    for b in (2, 1, 0):
        cols = pl.ds(b * T, T)
        for side, device in enumerate((above, below)):
            ghost_copies[b, side] = group()
            ghost_copies[b, side].put(gho.at[pl.ds(FACE * (1 - side), FACE), cols], gh.at[b, side], device)
    tell(0)

    for load in loads[:3]:
        load.wait()
    alive = jnp.where(iota((ms.shape[0], T), 0) < 3 * nv[0], 1.0, 0.0).astype(BF16)
    for q in range(4):
        ms[:, q * T : (q + 1) * T] = ms[:, q * T : (q + 1) * T] * alive

    for load in loads[3:]:
        load.wait()
    for j in range(4):
        acc = dot_rows(ev[:, 256 * j : 256 * (j + 1)], ms[...])
        for q in range(4):
            part[q, 2 * j : 2 * j + 2] = acc[:, q * T : (q + 1) * T].reshape(2, NH, NX, NC, K, T)
        if j == 1:
            told(0)
            tell(1)

    cores = {}

    def core_send(b):
        cores[b] = group()
        cores[b].put(part.at[b, :, :, :, 1 - c], cr.at[b], core)

    def core_sum(b):
        cores[b].arrive(cr.at[b])
        cs[b] = part[b, :, :, :, c] + cr[b]

    def over_x(src, dst, cut):
        copies = group()
        for n, xx in enumerate(x_peers):
            copies.put(cut(src, xx), dst.at[n], dev(x=xx))
        return copies

    def over_y(src, dst):
        copies = group()
        for n, yy in enumerate(y_peers):
            copies.put(src.at[yy], dst.at[n], dev(y=yy))
        return copies

    def over_h(src, dst):
        copies = group()
        copies.put(src, dst, h_peer)
        return copies

    def gather(copies, own, slots_of):
        copies.arrive(slots_of)
        for n in range(slots_of.shape[0]):
            own = own + slots_of[n]
        return own

    def code_over_x(i):
        block = cs[2 * i]
        scale = scale_of(block.reshape(512, T))
        for xx in range(NX):
            qx[i, xx, 0:128] = code(block[:, :, xx].reshape(128, T), scale)
            qx[i, xx, 128:144] = code_of(scale)
        return over_x(qx.at[i], rx.at[i], lambda ref, xx: ref.at[xx])

    def code_over_y():
        block = cs[1].reshape(512, T)
        scale = scale_of(block)
        qy[:, 0:64] = code(block, scale).reshape(NY, 64, T)
        for yy in range(NY):
            qy[yy, 64:80] = code_of(scale)
        return over_y(qy, ryb)

    def code_over_h():
        block = cs[3, :, 1 - h].reshape(256, T)
        scale = scale_of(block)
        qh[0:256] = code(block, scale)
        qh[256:272] = code_of(scale)
        return over_h(qh, rhc)

    def gather_coded(copies, own, slots_of):
        copies.arrive(slots_of)
        for n in range(slots_of.shape[0]):
            own = own + decode(slots_of[n])
        return own

    core_send(0)
    told(1)
    tell(2)

    for side in range(2):
        places[side].arrive(rs.at[side])
        rows = pl.ds(FACE * side, FACE)
        put = placing(rs[side], side)
        ep[rows, :] = dot_rows(put, ev[rows, :]).astype(BF16)
        vp[rows, :] = dot_rows(put, ms[rows, 0:T]).astype(BF16)
    core_sum(0)
    xs0 = code_over_x(0)
    told(2)
    pl.semaphore_signal(relay.at[3], 1, device_id=h_peer, device_id_type=MESH)

    def add_ghosts(b):
        for side in range(2):
            ghost_copies[b - 1, side].arrive(gh.at[b - 1, side])
        ghosts = gh[b - 1].reshape(2 * FACE, T)
        for j in range(4):
            now = dot_rows(ep[:, 256 * j : 256 * (j + 1)], ghosts).reshape(2, NH, NX, NC, K, T)
            part[b, 2 * j : 2 * j + 2] = part[b, 2 * j : 2 * j + 2] + now
        core_send(b)

    add_ghosts(3)
    add_ghosts(2)
    core_sum(3)
    hsc = code_over_h()
    add_ghosts(1)
    core_sum(2)
    xs2 = code_over_x(1)
    core_sum(1)
    ysb = code_over_y()

    total = dot_rows(ms[:, :T], ms[:, T:])
    diagonal = iota((T, T), 0) == iota((T, T), 1)
    parts = []
    for b in range(3):
        now = total[:, b * T : (b + 1) * T] + dot_rows(vp[...], gh[b].reshape(2 * FACE, T))
        parts.append(jnp.sum(jnp.where(diagonal, now, 0.0), axis=0, keepdims=True))
    tp[...] = jnp.concatenate(parts, axis=1)
    tot_core = group()
    tot_core.put(tp, tc, core)

    x1[0] = gather_coded(xs0, cs[0, :, :, x].reshape(128, T), rx.at[0]).reshape(NY, NH, K, T)
    ys0 = over_y(x1.at[0], ry.at[0])
    tot_core.arrive(tc)
    tx[x] = tp[...] + tc[...]
    tot_x = group()
    for xx in x_peers:
        tot_x.put(tx.at[x], tx.at[x], dev(x=xx))
    x1[1] = gather_coded(xs2, cs[2, :, :, x].reshape(128, T), rx.at[1]).reshape(NY, NH, K, T)
    ys2 = over_y(x1.at[1], ry.at[1])
    hsc.arrive(rhc)
    h1c[...] = cs[3, :, h] + decode(rhc[...]).reshape(NY, NX, K, T)
    xsc = over_x(h1c, rxc, lambda ref, xx: ref.at[:, xx])
    tot_x.arrive(tx.at[pl.ds(0, 3)])
    ty[y] = ((tx[0] + tx[1]) + tx[2]) + tx[3]
    tot_y = group()
    for yy in y_peers:
        tot_y.put(ty.at[y], ty.at[y], dev(y=yy))
    y1b[...] = gather_coded(ysb, cs[1, y].reshape(64, T), ryb).reshape(NH, NX, K, T)
    pl.semaphore_wait(relay.at[3], 1)
    xsb = group()
    for n, (hh, xx) in enumerate(hx_peers):
        xsb.put(y1b.at[hh, xx], rxb.at[n], dev(h=hh, x=xx))
    x1c[...] = gather(xsc, h1c[:, x], rxc)
    ysc = over_y(x1c, ryc)
    rr[0] = gather(ys0, x1[0, y], ry.at[0])
    hs0 = over_h(rr.at[0, 1 - h], rh.at[0])
    tot_y.arrive(ty.at[pl.ds(0, 7)])
    summed = ty[0]
    for n in range(1, NY):
        summed = summed + ty[n]
    th[0] = summed
    tot_h = over_h(th.at[0], th.at[1])
    rr[1] = gather(ys2, x1[1, y], ry.at[1])
    hs2 = over_h(rr.at[1, 1 - h], rh.at[1])
    last = gather(ysc, x1c[y], ryc)
    hs0.arrive(rh.at[0])
    hs2.arrive(rh.at[1])
    final = [rr[0, h] + rh[0], gather(xsb, y1b[h, x], rxb), rr[1, h] + rh[1], last]
    flux = jnp.concatenate([final[0] * final[1 + b] for b in range(3)], axis=1)

    here = z * NC + c
    sz[here] = jnp.sum(flux, axis=0, keepdims=True)
    szs = group()
    for zz, cc in z_peers:
        szs.put(sz.at[here], sz.at[here], dev(h=lax.div(zz, NM), m=lax.rem(zz, NM), c=cc))
    tot_h.arrive(th.at[1])
    lagged = hankel((th[0] + th[1]) * (1.0 / math.sqrt(ms.shape[0] // 3 * domains)))
    for b in range(3):
        out[b] = flux[:, b * T : (b + 1) * T]
    out[3] = correlate(flux, lagged)
    for copies in places + list(ghost_copies.values()) + list(cores.values()):
        copies.left()
    for copies in (xs0, ys0, hs0, ysb, xsb, xs2, ys2, hs2, hsc, xsc, ysc):
        copies.left()
    for copies in (tot_core, tot_x, tot_y, tot_h):
        copies.left()
    szs.arrive(sz.at[pl.ds(0, 15)])
    summed = sz[0]
    for n in range(1, 16):
        summed = summed + sz[n]
    there = y * NX + x
    sp[there] = summed
    sps = group()
    for yy, xx in p_peers:
        sps.put(sp.at[there], sp.at[there], dev(y=yy, x=xx))
    szs.left()
    sps.arrive(sp.at[pl.ds(0, 31)])
    slab = sp[0]
    for n in range(1, 32):
        slab = slab + sp[n]
    out[4] = correlate(jnp.broadcast_to(slab, (8, 3 * T)), lagged) * (1.0 / math.sqrt(NM * domains * K))
    sps.left()


def deliver(held, flux, corr, slab):
    flux[0] = held[0:3]
    corr[0] = held[3, :, :LAGS]
    slab[...] = held[4, 0:1, :LAGS]


def per_device(velocity, local_virial, ghost_virial, eigvec, ghost_slot, counts):
    rows, modes = eigvec.shape
    vmem = pltpu.VMEM
    dma = pltpu.SemaphoreType.DMA
    scratch = [
        vmem((rows, modes), BF16),
        vmem((rows, 4 * T), BF16),
        pltpu.SMEM((1,), jnp.int32),
        vmem((2, 1, T), jnp.int32),
        vmem((3, 2, FACE, T), BF16),
        vmem((2 * FACE, modes), BF16),
        vmem((2 * FACE, T), BF16),
        vmem((4, NY, NH, NX, NC, K, T), F32),
        vmem((4, NY, NH, NX, K, T), F32),
        vmem((4, NY, NH, NX, K, T), F32),
        vmem((2, NX, 144, T), I16),
        vmem((NY, 80, T), I16),
        vmem((272, T), I16),
        vmem((2, 3, 144, T), I16),
        vmem((2, NY, NH, K, T), F32),
        vmem((2, NY - 1, NH, K, T), F32),
        vmem((2, NH, K, T), F32),
        vmem((2, K, T), F32),
        vmem((NY - 1, 80, T), I16),
        vmem((NH, NX, K, T), F32),
        vmem((7, K, T), F32),
        vmem((272, T), I16),
        vmem((NY, NX, K, T), F32),
        vmem((3, NY, K, T), F32),
        vmem((NY, K, T), F32),
        vmem((NY - 1, K, T), F32),
        vmem((1, 3 * T), F32),
        vmem((1, 3 * T), F32),
        vmem((NX, 1, 3 * T), F32),
        vmem((NY, 1, 3 * T), F32),
        vmem((2, 1, 3 * T), F32),
        vmem((16, 1, 3 * T), F32),
        vmem((32, 1, 3 * T), F32),
        dma((7,)),
        dma((2, 32)),
        pltpu.SemaphoreType.REGULAR((4,)),
    ]
    held = pl.pallas_call(
        kernel,
        out_shape=jax.ShapeDtypeStruct((5, K, T), F32),
        in_specs=[pl.BlockSpec(memory_space=pltpu.HBM)] * 6,
        out_specs=pl.BlockSpec(memory_space=vmem),
        scratch_shapes=scratch,
        compiler_params=pltpu.CompilerParams(
            collective_id=0, has_side_effects=True, vmem_limit_bytes=56 * 2**20
        ),
        name="green_kubo",
    )(velocity, local_virial, ghost_virial, eigvec, ghost_slot.reshape(1, T), counts)
    flux, corr, slab = pl.pallas_call(
        deliver,
        out_shape=(
            jax.ShapeDtypeStruct((1, 3, K, T), F32),
            jax.ShapeDtypeStruct((1, K, LAGS), F32),
            jax.ShapeDtypeStruct((1, LAGS), F32),
        ),
        name="deliver",
    )(held)
    return jnp.transpose(flux, (0, 2, 1, 3)), corr, slab.reshape(LAGS)


def solution(mesh):
    return jax.shard_map(
        per_device,
        mesh=mesh,
        in_specs=(
            P("atom", None),
            P("atom", None),
            P("atom", None),
            P("atom", "mode"),
            P("atom"),
            P("atom"),
        ),
        out_specs=(P("mode", "atom", None, None), P("mode", "atom", None), P()),
        check_vma=False,
    )
```
